128 devices in a mesh: seq: 2 (over x_hi), fsdp: 64 (over y, z, x_lo, core).
Axes of the slice: x: 4 (x_hi: 2, x_lo: 2; x = x_hi * 2 + x_lo), y: 4, z: 4, core: 2. Of those that a mesh axis runs over, the one named last changes fastest.
Arguments:
- tokens: bfloat16 [64, 256, 2048], P('fsdp', 'seq'), may hold values from -6 to 6
- gain_attn: bfloat16 [2048], P(('seq', 'fsdp')), may hold values from 0.5 to 1.5
- w_query: bfloat16 [2048, 2048], P(('seq', 'fsdp')), may hold values from -0.1875 to 0.1875
- w_key: bfloat16 [2048, 256], P(('seq', 'fsdp')), may hold values from -0.1875 to 0.1875
- w_value: bfloat16 [2048, 256], P(('seq', 'fsdp')), may hold values from -0.125 to 0.125
- w_out: bfloat16 [2048, 2048], P(('seq', 'fsdp')), may hold values from -0.75 to 0.75
- gain_mlp: bfloat16 [2048], P(('seq', 'fsdp')), may hold values from 0.5 to 1.5
- w_gate: bfloat16 [2048, 5632], P(('seq', 'fsdp')), may hold values from -0.125 to 0.125
- w_up: bfloat16 [2048, 5632], P(('seq', 'fsdp')), may hold values from -0.125 to 0.125
- w_down: bfloat16 [2048, 5632], P(('seq', 'fsdp')), may hold values from -0.078125 to 0.078125
- cotangent: bfloat16 [64, 256, 2048], P('fsdp', 'seq'), may hold values from -16 to 16
Outputs:
- block_output: bfloat16 [64, 256, 2048], P('fsdp', 'seq')
- input_grad: float32 [64, 256, 2048], P('fsdp', 'seq')
- gain_attn_grad: float32 [2048], P(('seq', 'fsdp'))
- query_grad: float32 [2048, 2048], P(('seq', 'fsdp'))
- key_grad: float32 [2048, 256], P(('seq', 'fsdp'))
- value_grad: float32 [2048, 256], P(('seq', 'fsdp'))
- out_grad: float32 [2048, 2048], P(('seq', 'fsdp'))
- gain_mlp_grad: float32 [2048], P(('seq', 'fsdp'))
- gate_grad: float32 [2048, 5632], P(('seq', 'fsdp'))
- up_grad: float32 [2048, 5632], P(('seq', 'fsdp'))
- down_grad: float32 [2048, 5632], P(('seq', 'fsdp'))
The draws below stay inside these ranges and needn't reach their ends.
All inputs are finite; a program needn't handle non-finite values.
Results may differ from the reference program's by a relative error of at most 0.013.
The reference program's roundings to bfloat16 on the way count: a program that leaves them out, or rounds other values in their place, can miss the bound.
Values may be sent and summed in bfloat16 or wider, within the bound.
No kernel may reach another device: no remote copies, remote signals or barrier semaphores. Data moves between devices by JAX's collectives and lax.ppermute only.
A program may use at most 704 MiB of HBM per device.

```python
import jax
import jax.numpy as jnp
from jax import lax

D = 2048
HEADS = 32
KV_HEADS = 4
HEAD_DIM = 64
FF = 5632
SEQS = 64
LENGTH = 256
BLOCK = 256


def strengthened(drawn, stream_key, source, target, shards_of, factor):
    def block_of(axis_at):
        return (jnp.arange(drawn.shape[axis_at]) // (drawn.shape[axis_at] // shards_of)).reshape((-1,) + (1,) * (drawn.ndim - 1 - axis_at))

    near = jax.random.permutation(stream_key, shards_of)[block_of(target)]
    other_side = (block_of(target) + shards_of // 2) % shards_of
    return jnp.where((block_of(source) == near) | (block_of(source) == other_side), factor * drawn, drawn)


def levels(rng, dims, split, least, largest):
    gain, own = 1.0, jax.random.fold_in(rng, 6)
    for dim, blocks in split:
        steps = jnp.exp(jax.random.uniform(jax.random.fold_in(own, dim), (blocks,), jnp.float32, least / len(split), largest / len(split)))
        gain = gain * jnp.repeat(steps, dims[dim] // blocks).reshape([-1 if axis == dim else 1 for axis in range(len(dims))])
    return gain


def centred(stream_key, shape, deviation, limit, shards=(), held_as=jnp.bfloat16):
    loudness = levels(stream_key, shape, shards, -0.22, 0.18) if shards else 1.0
    entries = jax.random.normal(stream_key, shape, jnp.float32) * deviation * loudness
    return jnp.minimum(jnp.maximum(entries, -limit), limit).astype(held_as)


def bell_draw_with(key, dims, deviation, limit, shards, heavy, kind=jnp.bfloat16):
    values = deviation * jax.random.normal(key, dims, jnp.float32)
    if shards:
        values = values * levels(key, dims, shards, -0.22, 0.18)
    return jnp.clip(strengthened(values, jax.random.fold_in(key, 3), *heavy), -limit, limit).astype(kind)


def setup_inputs(seed: int = 0) -> dict:
    seeds = jax.random.split(jax.random.key(seed), 12)
    return {
        "tokens": centred(seeds[0], (SEQS, LENGTH, D), 1.0, 6.0, ((0, 64), (1, 2))),
        "gain_attn": jnp.clip(1.0 + 0.1 * jax.random.normal(seeds[1], (D,), jnp.float32), 0.5, 1.5).astype(jnp.bfloat16),
        "w_query": centred(seeds[2], (D, D), (D // 2) ** -0.5, 0.1875, ((0, 128),)),
        "w_key": centred(seeds[3], (D, KV_HEADS * HEAD_DIM), (D // 2) ** -0.5, 0.1875, ((0, 128),)),
        "w_value": centred(seeds[4], (D, KV_HEADS * HEAD_DIM), D ** -0.5, 0.125, ((0, 128),)),
        "w_out": centred(seeds[5], (D, D), (D // 32) ** -0.5, 0.75, ((0, 128),)),
        "gain_mlp": jnp.clip(1.0 + 0.1 * jax.random.normal(seeds[6], (D,), jnp.float32), 0.5, 1.5).astype(jnp.bfloat16),
        "w_gate": centred(seeds[7], (D, FF), D ** -0.5, 0.125, ((0, 128),)),
        "w_up": centred(seeds[8], (D, FF), D ** -0.5, 0.125, ((0, 128),)),
        "w_down": centred(seeds[9], (D, FF), FF ** -0.5, 0.078125, ((0, 128),)),
        "cotangent": bell_draw_with(seeds[10], (SEQS, LENGTH, D), 1.0, 16.0, ((0, 64), (1, 2)), (0, 2, 64, 4.0)),
    }


EPS = 1e-05
NEG = -1e+30

@jax.custom_vjp
def low(v):
    return lax.optimization_barrier(v.astype(jnp.bfloat16)).astype(jnp.float32)

@jax.custom_vjp
def low_back(v):
    return v

def low_keep(v):
    return (low(v), None)

def low_pass(kept, grad):
    return (grad,)

def back_keep(v):
    return (v, None)

def back_low(kept, grad):
    return (low(grad),)
low.defvjp(low_keep, low_pass)
low_back.defvjp(back_keep, back_low)

def exact_dot(earlier, latest):
    return jnp.dot(earlier, latest, precision=lax.Precision.HIGHEST)

def rotary_tables(length, width):
    half_width = width // 2
    frequency = 10000.0 ** (-2.0 * jnp.arange(half_width, dtype=jnp.float32) / width)
    angles = jnp.arange(length, dtype=jnp.float32)[:, None] * frequency[None, :]
    angles = jnp.concatenate([angles, angles], axis=1)
    return (jnp.cos(angles), jnp.sin(angles))

def rotate_half(values):
    half_width = values.shape[-1] // 2
    return jnp.concatenate([-values[..., half_width:], values[..., :half_width]], axis=-1)

def rotary(values, cosine_table, sine_table):
    return values * cosine_table[:, None, :] + rotate_half(values) * sine_table[:, None, :]

def block_forward(inputs, weights):
    gain_attn, w_query, w_key, w_value, w_out, gain_mlp, w_gate, w_up, w_down = weights
    length = inputs.shape[0]
    group_size = HEADS // KV_HEADS
    scale_one = lax.rsqrt(lax.optimization_barrier(jnp.mean(inputs * inputs, axis=1, keepdims=True)) + EPS)
    xn_one = low(inputs * scale_one * gain_attn)
    query_proj = low_back(low(exact_dot(xn_one, w_query)))
    key_proj = low_back(low(exact_dot(xn_one, w_key)))
    value_proj = low_back(low(exact_dot(xn_one, w_value)))
    cosine_table, sine_table = rotary_tables(length, HEAD_DIM)
    query_rot = low(rotary(query_proj.reshape(length, HEADS, HEAD_DIM), cosine_table, sine_table))
    key_rot = low(rotary(key_proj.reshape(length, KV_HEADS, HEAD_DIM), cosine_table, sine_table))
    value_heads = value_proj.reshape(length, KV_HEADS, HEAD_DIM)
    query_blocks = query_rot.reshape(length // BLOCK, BLOCK, KV_HEADS, group_size, HEAD_DIM)
    key_places = jnp.arange(length)

    def attend(block_pair):
        query_block, first_row = block_pair
        scores = jnp.einsum('qcgd,kcd->cgqk', query_block, key_rot, precision=lax.Precision.HIGHEST) * HEAD_DIM ** (-0.5)
        scores = low_back(scores)
        query_rows = first_row + jnp.arange(BLOCK)
        allowed = key_places[None, :] <= query_rows[:, None]
        scores = jnp.where(allowed, scores, NEG)
        attn_probs = jax.nn.softmax(scores, axis=-1)
        mixed = jnp.einsum('cgqk,kcd->qcgd', low(attn_probs), value_heads, precision=lax.Precision.HIGHEST)
        return low_back(low(mixed.reshape(BLOCK, D)))
    first_rows = jnp.arange(length // BLOCK) * BLOCK
    attended = lax.map(jax.checkpoint(attend), (query_blocks, first_rows)).reshape(length, D)
    branch_attn = low_back(exact_dot(attended, w_out))
    resid = inputs + branch_attn
    scale_two = lax.rsqrt(lax.optimization_barrier(jnp.mean(resid * resid, axis=1, keepdims=True)) + EPS)
    xn_two = low(resid * scale_two * gain_mlp)
    gate_value = low_back(exact_dot(xn_two, w_gate))
    up_value = low_back(exact_dot(xn_two, w_up))
    hidden = low(jax.nn.silu(gate_value) * up_value)
    branch_mlp = low_back(exact_dot(hidden, w_down.T))
    return resid + branch_mlp

def reference(tokens, gain_attn, w_query, w_key, w_value, w_out, gain_mlp, w_gate, w_up, w_down, cotangent):
    weights = tuple((member.astype(jnp.float32) for member in (gain_attn, w_query, w_key, w_value, w_out, gain_mlp, w_gate, w_up, w_down)))

    def sequence_step(summed, sequence_pair):
        sequence_in, sequence_cot = sequence_pair
        output, pullback = jax.vjp(block_forward, sequence_in.astype(jnp.float32), weights)
        grad_input, grad_weights = pullback(sequence_cot.astype(jnp.float32))
        summed = tuple((earlier + latest for earlier, latest in zip(summed, grad_weights)))
        return (summed, (output.astype(jnp.bfloat16), grad_input))
    empty_sum = tuple((jnp.zeros_like(member) for member in weights))
    summed, (block_output, input_grad) = lax.scan(sequence_step, empty_sum, (tokens, cotangent))
    return (block_output, input_grad, summed[0], summed[1], summed[2], summed[3], summed[4], summed[5], summed[6], summed[7], summed[8])
```

```python
import functools

import jax
import jax.numpy as jnp
from jax import lax
from jax.experimental import pallas as pl
from jax.experimental.pallas import tpu as pltpu
from jax.sharding import Mesh, PartitionSpec as P

HEADS = 32
KV_HEADS = 4
HEAD_DIM = 64
EPS = 1e-05
NEG = -1e30
LENGTH = 256
HALF = 128
MIB = 1024 * 1024

AXES = ("xh", "y", "z", "xl", "c")
SIZES = (2, 4, 4, 2, 2)
CHIP_X = ("xh", "xl")
GROUP = ("xl", "xh", "c")
MEMBERS = 8
PAIRED = ("xh", "c")
PLANE = ("y", "z")

bf16 = jnp.bfloat16
f32 = jnp.float32


def contract(a, b, dim_a, dim_b):
    return lax.dot_general(a, b, (((dim_a,), (dim_b,)), ((), ())), preferred_element_type=f32)


def shift(values, axis, by, size):
    return lax.ppermute(values, axis, [(i, (i + by) % size) for i in range(size)])


def after(values, *earlier):
    return lax.optimization_barrier((values, *earlier))[0]


def regroup_kernel(back, in_ref, out_ref):
    for k in range(16):
        if back:
            tile = in_ref[:, 128 * k : 128 * (k + 1)]
            out_ref[:, 64 * k : 64 * k + 64] = jnp.concatenate([tile[:, :32], tile[:, 64:96]], axis=1)
            out_ref[:, 1024 + 64 * k : 1088 + 64 * k] = jnp.concatenate([tile[:, 32:64], tile[:, 96:]], axis=1)
        else:
            low = in_ref[:, 64 * k : 64 * k + 64]
            high = in_ref[:, 1024 + 64 * k : 1088 + 64 * k]
            out_ref[:, 128 * k : 128 * (k + 1)] = jnp.concatenate(
                [low[:, :32], high[:, :32], low[:, 32:], high[:, 32:]], axis=1
            )


def regroup(values, back=False):
    return pl.pallas_call(
        functools.partial(regroup_kernel, back),
        out_shape=jax.ShapeDtypeStruct(values.shape, values.dtype),
    )(values)


def pair_gather(rows):
    there = shift(rows, "xh", 1, 2)
    return (rows, there), (shift(rows, "c", 1, 2), shift(there, "c", 1, 2))


def pair_sum(own, other):
    half = own.shape[0] // 2
    mine = own.astype(f32) + shift(other, "c", 1, 2).astype(f32)
    return mine[:half] + shift(mine[half:].astype(bf16), "xh", 1, 2).astype(f32)


def group_gather(rows):
    own = [rows] + [shift(rows, CHIP_X, -ahead, 4) for ahead in (1, 2, 3)]
    return [(block, shift(block, "c", 1, 2)) for block in own]


def group_sum(terms):
    total = 0.0
    for ahead, (own, other) in terms:
        mine = own.astype(f32) + shift(other, "c", 1, 2).astype(f32)
        if ahead:
            mine = shift(mine.astype(bf16), CHIP_X, ahead, 4).astype(f32)
        total = total + mine
    return total


def plane_sum(terms):
    got = lax.all_to_all(terms, PLANE, 0, 0, tiled=True)
    return jnp.sum(got.astype(f32), axis=0)


def neighbour_gather(block):
    got = shift(block, "xl", 1, 2)
    first = lax.axis_index("xl") == 0
    return jnp.stack([jnp.where(first, block, got), jnp.where(first, got, block)])


def neighbour_sum(terms):
    first = lax.axis_index("xl") == 0
    kept = jnp.where(first, terms[0], terms[1])
    sent = jnp.where(first, terms[1], terms[0])
    return kept + shift(sent.astype(bf16), "xl", 1, 2).astype(f32)


def head_rows():
    pairs = []
    for a in range(2):
        for b in range(2):
            for z in range(4):
                for xl in range(2):
                    for c in range(2):
                        source = (((2 * a + b) * 4 + z) * 2 + xl) * 2 + c
                        to_y, to_z = 2 * b + z // 2, 2 * (z % 2) + xl
                        pairs.append((source, ((to_y * 4 + to_z) * 2 + c) * 2 + a))
    return pairs


FSDP = ("y", "z", "xl", "c")


def rms_scale(values):
    return lax.rsqrt(jnp.mean(values * values, axis=1, keepdims=True) + EPS)


def norm_back(grad_normed, normed, scale_rows, gain_full):
    scaled = grad_normed * gain_full
    return scale_rows * (scaled - normed * jnp.mean(scaled * normed, axis=1, keepdims=True))


def rotate_half(values):
    width = values.shape[1]
    lane = lax.broadcasted_iota(jnp.int32, values.shape, 1) % HEAD_DIM
    later = pltpu.roll(values, width - HEAD_DIM // 2, 1)
    earlier = pltpu.roll(values, HEAD_DIM // 2, 1)
    return jnp.where(lane < HEAD_DIM // 2, -later, earlier)


def head(values, h):
    return values[:, HEAD_DIM * h : HEAD_DIM * (h + 1)]


def allowed_places(first):
    shape = (LENGTH, LENGTH)
    rows = (lax.broadcasted_iota(jnp.int32, shape, 0) + first) & (LENGTH - 1)
    return ((lax.broadcasted_iota(jnp.int32, shape, 1) + first) & (LENGTH - 1)) <= rows


def probabilities(query, key, allowed):
    scores = jnp.where(allowed, contract(query, key, 1, 1) * HEAD_DIM**-0.5, NEG)
    exp_scores = jnp.exp(scores - jnp.max(scores, axis=1, keepdims=True))
    return exp_scores / jnp.sum(exp_scores, axis=1, keepdims=True)


def attend_kernel(first_ref, own_ref, there_ref, gain_ref, w_ref, out_w_ref, cos_ref, sin_ref, xn_ref, qkv_ref, mixed_ref, out_ref):
    inputs = jnp.concatenate([own_ref[...], there_ref[...]], axis=0).astype(f32)
    xn_ref[...] = (inputs * rms_scale(inputs) * gain_ref[...]).astype(bf16)
    proj = contract(xn_ref[...], w_ref[...], 1, 0).astype(bf16)
    query = proj[:, :512].astype(f32)
    query = (query * cos_ref[...] + rotate_half(query) * sin_ref[...]).astype(bf16)
    qkv_ref[:, :512] = query
    wide = proj[:, 512:].astype(f32)
    turned = wide * cos_ref[:, :128] + rotate_half(wide) * sin_ref[:, :128]
    lane = lax.broadcasted_iota(jnp.int32, wide.shape, 1)
    key_value = jnp.where(lane < HEAD_DIM, turned, wide).astype(bf16)
    qkv_ref[:, 512:] = key_value
    key, value = key_value[:, :HEAD_DIM], key_value[:, HEAD_DIM:]
    allowed = allowed_places(first_ref[0])
    mixed = [
        contract(probabilities(head(query, h), key, allowed).astype(bf16), value, 1, 0) for h in range(8)
    ]
    mixed_ref[...] = jnp.concatenate(mixed, axis=1).astype(bf16)
    out_ref[...] = contract(mixed_ref[...], out_w_ref[...], 1, 0).astype(bf16)


def attend_back_kernel(first_ref, own_ref, there_ref, w_ref, out_w_ref, cos_ref, sin_ref, qkv_ref, out_ref, back_ref):
    grad = jnp.concatenate([own_ref[...], there_ref[...]], axis=0)
    grad = contract(grad, out_w_ref[...], 1, 1).astype(bf16)
    query = qkv_ref[:, :512]
    key_value = qkv_ref[:, 512:]
    key, value = key_value[:, :HEAD_DIM], key_value[:, HEAD_DIM:]
    allowed = allowed_places(first_ref[0])
    grad_key = jnp.zeros((LENGTH, HEAD_DIM), f32)
    grad_value = jnp.zeros((LENGTH, HEAD_DIM), f32)
    grad_query = []
    for h in range(8):
        probs = probabilities(head(query, h), key, allowed)
        grad_probs = contract(head(grad, h), value, 1, 1)
        delta = jnp.sum(probs * grad_probs, axis=1, keepdims=True)
        grad_scores = (probs * (grad_probs - delta)).astype(bf16)
        grad_query.append(contract(grad_scores, key, 1, 0))
        grad_key = grad_key + contract(grad_scores, head(query, h), 0, 0)
        grad_value = grad_value + contract(probs.astype(bf16), head(grad, h), 0, 0)
    grad_query = jnp.concatenate(grad_query, axis=1) * HEAD_DIM**-0.5
    out_ref[:, :512] = (grad_query * cos_ref[...] - rotate_half(grad_query * sin_ref[...])).astype(bf16)
    wide = jnp.concatenate([grad_key * HEAD_DIM**-0.5, grad_value], axis=1)
    turned = wide * cos_ref[:, :128] - rotate_half(wide * sin_ref[:, :128])
    lane = lax.broadcasted_iota(jnp.int32, wide.shape, 1)
    out_ref[:, 512:] = jnp.where(lane < HEAD_DIM, turned, wide).astype(bf16)
    back_ref[...] = contract(out_ref[...], w_ref[...], 1, 1).astype(bf16)


def call(kernel, outs, flops, *arrays, grid=(), in_specs=None, out_specs=None):
    vmem = pl.BlockSpec(memory_space=pltpu.VMEM)
    smem = pl.BlockSpec(memory_space=pltpu.SMEM)
    return pl.pallas_call(
        kernel,
        out_shape=[jax.ShapeDtypeStruct(shape, bf16) for shape in outs],
        grid=grid,
        in_specs=in_specs or [smem if a.dtype == jnp.int32 else vmem for a in arrays],
        out_specs=out_specs or [vmem] * len(outs),
        compiler_params=pltpu.CompilerParams(vmem_limit_bytes=32 * MIB),
        cost_estimate=pl.CostEstimate(flops=flops, bytes_accessed=8 * MIB, transcendentals=1 << 19),
    )(*arrays)


def mlp_kernel(part, own_ref, other_ref, own_cot_ref, other_cot_ref, w_ref, hidden_ref, grad_ref, back_ref, back_other_ref):
    xn = jnp.concatenate([own_ref[...], other_ref[...]], axis=0)
    cot = jnp.concatenate([own_cot_ref[...], other_cot_ref[...]], axis=0)
    wide = contract(xn, w_ref[:, : 2 * part], 1, 0)
    grad_hidden = contract(cot, w_ref[:, 2 * part :], 1, 0)
    gate, up = wide[:, :part], wide[:, part:]
    sigmoid_gate = jax.nn.sigmoid(gate)
    silu_gate = gate * sigmoid_gate
    hidden_ref[...] = (silu_gate * up).astype(bf16)
    grad_ref[:, :part] = (
        grad_hidden * up * (sigmoid_gate * (1.0 + gate * (1.0 - sigmoid_gate)))
    ).astype(bf16)
    grad_ref[:, part:] = (grad_hidden * silu_gate).astype(bf16)
    back = contract(grad_ref[...], w_ref[:, : 2 * part], 1, 1).astype(bf16)
    rows = own_ref.shape[0]
    back_ref[...] = back[:rows]
    back_other_ref[...] = back[rows:]


def mlp_out_kernel(part, *refs):
    hidden_refs, w_ref, out_refs = refs[:4], refs[4], refs[5:]
    down = w_ref[:, 2 * part :]
    for chip in range(4):
        out = contract(hidden_refs[chip][...], down, 1, 1).astype(bf16)
        rows = out.shape[0] // 2
        out_refs[2 * chip][...] = out[:rows]
        out_refs[2 * chip + 1][...] = out[rows:]


def mlp_terms_kernel(part, *refs):
    xn, cot, grad, hidden = [
        jnp.concatenate([ref[...] for ref in group], axis=0) for group in (refs[:8], refs[8:16], refs[16:20], refs[20:24])
    ]
    out_ref = refs[24]
    out_ref[:, : 2 * part] = contract(xn, grad, 0, 0).astype(bf16)
    out_ref[:, 2 * part :] = contract(cot, hidden, 0, 0).astype(bf16)


def columns_spec(rows, block):
    return pl.BlockSpec((rows, block), lambda i: (0, i))


def whole_spec(array):
    return pl.BlockSpec(array.shape, lambda i: (0, 0), pipeline_mode=pl.Buffered(1))


def mlp_terms(part, xn, cot, grad, hidden):
    rows, width = xn[0].shape
    block = 256
    return call(
        functools.partial(mlp_terms_kernel, part),
        [(width, 3 * part)],
        6 * 8 * rows * width * part,
        *xn,
        *cot,
        *grad,
        *hidden,
        grid=(width // block,),
        in_specs=[columns_spec(rows, block)] * 16 + [whole_spec(a) for a in grad + hidden],
        out_specs=[pl.BlockSpec((block, 3 * part), lambda i: (i, 0))],
    )[0]


def out_terms_kernel(mixed_ref, mixed_other_ref, *refs):
    own, other = [jnp.concatenate([ref[...] for ref in pair], axis=0) for pair in (refs[:2], refs[2:4])]
    refs[4][...] = (contract(mixed_ref[...], own, 0, 0) + contract(mixed_other_ref[...], other, 0, 0)).astype(bf16)


def out_terms(mixed, grad):
    rows, width = grad[0][0].shape
    block = 512
    blocks = [columns_spec(rows, block)] * 4
    return call(
        out_terms_kernel,
        [(512, width)],
        8 * rows * width * 512,
        *mixed,
        *grad[0],
        *grad[1],
        grid=(width // block,),
        in_specs=[whole_spec(a) for a in mixed] + blocks,
        out_specs=[columns_spec(512, block)],
    )[0]


def qkv_terms_kernel(xn_ref, xn_other_ref, grad_ref, grad_other_ref, out_ref):
    out_ref[...] = (
        contract(xn_ref[...], grad_ref[...], 0, 0) + contract(xn_other_ref[...], grad_other_ref[...], 0, 0)
    ).astype(bf16)


def qkv_terms(xn, grad):
    rows, width = xn[0].shape
    block = 512
    return call(
        qkv_terms_kernel,
        [(width, 640)],
        4 * rows * width * 640,
        *xn,
        *grad,
        grid=(width // block,),
        in_specs=[columns_spec(rows, block)] * 2 + [whole_spec(a) for a in grad],
        out_specs=[pl.BlockSpec((block, 640), lambda i: (i, 0))],
    )[0]


def rotary_tables(first):
    half = HEAD_DIM // 2
    frequency = 10000.0 ** (-2.0 * jnp.arange(half, dtype=f32) / HEAD_DIM)
    places = (jnp.arange(LENGTH) + first) % LENGTH
    angles = places[:, None].astype(f32) * frequency[None, :]
    return jnp.tile(jnp.cos(angles), (1, 16)), jnp.tile(jnp.sin(angles), (1, 16))


def on_device(
    tokens, gain_attn, w_query, w_key, w_value, w_out, gain_mlp, w_gate, w_up, w_down, cotangent
):
    own_rows = w_query.shape[0]
    part = w_gate.shape[1] // MEMBERS

    def for_members(members, *weights):
        blocks = [w.reshape(own_rows, members, -1) for w in weights]
        return jnp.concatenate(blocks, axis=2).swapaxes(0, 1)

    block = for_members(4, w_query, w_key, w_value)
    gains = jnp.concatenate([gain_attn, gain_mlp])[None, :]
    gains = jnp.broadcast_to(jnp.pad(gains, ((0, 7), (0, 640 - 2 * own_rows)))[None], (4, 8, 640))
    block = jnp.concatenate([block, gains], axis=1)
    block = lax.all_to_all(jnp.concatenate([block, block], axis=0), GROUP, 0, 0, tiled=True)
    gains = block[:, own_rows, : 2 * own_rows].reshape(1, MEMBERS * 2 * own_rows)
    out_block = neighbour_gather(lax.ppermute(regroup(w_out), FSDP, head_rows())).reshape(2 * own_rows, 2048)
    out_block = jnp.pad(out_block, ((0, 0), (0, 4 * 640 - 2048)))
    attn_block = jnp.concatenate(
        [
            block[:, :own_rows].reshape(MEMBERS * own_rows, 640),
            jnp.pad(gains, ((0, 7), (0, 640 - MEMBERS * 2 * own_rows))),
        ]
        + [out_block[:, 640 * j : 640 * (j + 1)] for j in range(4)],
        axis=0,
    )
    full = lax.all_gather(attn_block, PLANE, axis=0)
    attn_w = full[:, : MEMBERS * own_rows].reshape(2048, 640)
    gains = full[:, MEMBERS * own_rows, : MEMBERS * 2 * own_rows].reshape(16, MEMBERS, 2, own_rows).astype(f32)
    gain_one = gains[:, :, 0].reshape(1, 2048)
    gain_two = gains[:, :, 1].reshape(1, 2048)
    start = MEMBERS * own_rows + 8
    out_w = jnp.concatenate(
        [full[:, start + 2 * own_rows * j : start + 2 * own_rows * (j + 1)].reshape(512, 640) for j in range(4)], axis=1
    )[:, :2048]

    own_tokens = regroup(tokens[0])
    pair_tokens = pair_gather(own_tokens)

    mlp_block = after(for_members(MEMBERS, w_gate, w_up, w_down), attn_block)
    mlp_block = lax.all_to_all(mlp_block, GROUP, 0, 0, tiled=True).reshape(MEMBERS * own_rows, 3 * part)
    mlp_w = lax.all_gather(mlp_block, PLANE, axis=0, tiled=True)

    own_cotangent = regroup(cotangent[0])
    group_cotangent = group_gather(after(own_cotangent, pair_tokens))

    first = (HALF * lax.axis_index("xh")).astype(jnp.int32)
    cosine, sine = rotary_tables(first)
    first = first[None]

    def attend(chunks):
        shapes = [(LENGTH, 2048), (LENGTH, 640), (LENGTH, 512), (LENGTH, 2048)]
        return call(attend_kernel, shapes, 3 << 29, first, *chunks, gain_one, attn_w, out_w, cosine, sine)

    xn_other, qkv_other, mixed_other, out_other = attend(pair_tokens[1])
    xn_own, qkv_own, mixed_own, out_own = attend(pair_tokens[0])
    own_inputs = own_tokens.astype(f32)
    resid = own_inputs + pair_sum(out_own, after(out_other, group_cotangent))

    scale_two = rms_scale(resid)
    normed_two = resid * scale_two
    xn_two = group_gather((normed_two * gain_two).astype(bf16))

    hidden, grad_wide, back = [None] * 4, [None] * 4, []
    for chip in (0, 1, 3, 2):
        shapes = [(LENGTH, part), (LENGTH, 2 * part), (HALF, 2048), (HALF, 2048)]
        hidden[chip], grad_wide[chip], own, other = call(
            functools.partial(mlp_kernel, part), shapes, 10 * LENGTH * 2048 * part, *xn_two[chip], *group_cotangent[chip], mlp_w
        )
        back.append((chip, (own, other)))
    grad_xn_two = group_sum(back)

    flat = [[block for pair in pairs for block in pair] for pairs in (xn_two, group_cotangent)]
    shares = lax.psum_scatter(
        mlp_terms(part, *flat, grad_wide, hidden), PLANE, scatter_dimension=0, tiled=True
    )
    outs = call(
        functools.partial(mlp_out_kernel, part), [(HALF, 2048)] * 8, 8 * LENGTH * 2048 * part, *hidden, mlp_w
    )

    grad_resid = own_cotangent.astype(f32) + norm_back(grad_xn_two, normed_two, scale_two, gain_two)
    grad_attn = pair_gather(grad_resid.astype(bf16))

    def attend_back(chunks, qkv):
        shapes = [(LENGTH, 640), (LENGTH, 2048)]
        return call(attend_back_kernel, shapes, 5 << 29, first, *chunks, attn_w, out_w, cosine, sine, qkv)

    grad_other, back_other = attend_back(grad_attn[1], qkv_other)
    grad_own, back_own = attend_back(grad_attn[0], qkv_own)
    grad_xn_one = pair_sum(back_own, back_other)
    outs = after(outs, grad_attn)
    block_output = resid + group_sum([(chip, outs[2 * chip : 2 * chip + 2]) for chip in range(4)])

    scale_one = rms_scale(own_inputs)
    input_grad = grad_resid + norm_back(grad_xn_one, own_inputs * scale_one, scale_one, gain_one)

    out_term = out_terms((mixed_own, mixed_other), grad_attn).reshape(16, 2 * own_rows, 2048)
    out_share = neighbour_sum(plane_sum(out_term).reshape(2, own_rows, 2048))
    back_rows = [(there, here) for here, there in head_rows()]
    out_grad = regroup(lax.ppermute(out_share.astype(bf16), FSDP, back_rows).astype(f32), back=True)

    def from_members(share, axes):
        share = share.astype(bf16).reshape(-1, own_rows, share.shape[-1])
        return lax.all_to_all(share, axes, 0, 0, tiled=True).astype(f32)

    def join(parts):
        return parts.swapaxes(0, 1).reshape(own_rows, -1)

    attn_term = qkv_terms((xn_own, xn_other), (grad_own, grad_other)).reshape(16, 8 * own_rows, 640)
    attn_share = neighbour_sum(plane_sum(attn_term).reshape(2, 4 * own_rows, 640))
    attn_share = from_members(attn_share, PAIRED)
    query_grad = join(attn_share[:, :, :512])
    key_grad = join(attn_share[:, :, 512 : 512 + HEAD_DIM])
    value_grad = join(attn_share[:, :, 512 + HEAD_DIM :])

    shares = from_members(shares, GROUP)
    gate_grad = join(shares[:, :, :part])
    up_grad = join(shares[:, :, part : 2 * part])
    down_grad = join(shares[:, :, 2 * part :])

    def gain_grad(gain, *pairs):
        total = sum(jnp.sum(w.astype(f32) * grad, axis=1) for w, grad in pairs)
        return total / gain.astype(f32)

    gain_attn_grad = gain_grad(gain_attn, (w_query, query_grad), (w_key, key_grad), (w_value, value_grad))
    gain_mlp_grad = gain_grad(gain_mlp, (w_gate, gate_grad), (w_up, up_grad))
    return (
        regroup(block_output.astype(bf16), back=True)[None],
        regroup(input_grad, back=True)[None],
        gain_attn_grad,
        query_grad,
        key_grad,
        value_grad,
        out_grad,
        gain_mlp_grad,
        gate_grad,
        up_grad,
        down_grad,
    )


def solution(mesh):
    view = Mesh(mesh.devices.reshape(SIZES), AXES)
    split = P(("xh",) + FSDP)
    rows = P(("xh",) + FSDP, None)
    data = P(FSDP, "xh", None)
    return jax.shard_map(
        on_device,
        mesh=view,
        in_specs=(data, split, rows, rows, rows, rows, split, rows, rows, rows, data),
        out_specs=(data, data, split, rows, rows, rows, rows, split, rows, rows, rows),
        check_vma=False,
    )
```

```python
import functools

import jax
import jax.numpy as jnp
import numpy as np
from jax import lax
from jax.experimental import pallas as pl
from jax.experimental.pallas import tpu as pltpu
from jax.sharding import Mesh, PartitionSpec as P

HEADS = 32
KV_HEADS = 4
HEAD_DIM = 64
EPS = 1e-05
NEG = -1e30
LENGTH = 256
HALF = 128
MIB = 1024 * 1024
M_FLOPS = 1 << 20

AXES = ("xh", "y", "z", "xl", "c")
SIZES = (2, 4, 4, 2, 2)
CHIP_X = ("xh", "xl")
GROUP = ("xl", "xh", "c")
MEMBERS = 8
PAIRED = ("xh", "c")
PLANE = ("y", "z")

bf16 = jnp.bfloat16
f32 = jnp.float32


def contract(a, b, dim_a, dim_b):
    return lax.dot_general(a, b, (((dim_a,), (dim_b,)), ((), ())), preferred_element_type=f32)


def shift(values, axis, by, size):
    return lax.ppermute(values, axis, [(i, (i + by) % size) for i in range(size)])


def together(*values):
    return lax.optimization_barrier(values)


def regroup_to(out_ref, values):
    for k in range(16):
        low = values[:, 64 * k : 64 * k + 64]
        high = values[:, 1024 + 64 * k : 1088 + 64 * k]
        out_ref[:, 128 * k : 128 * (k + 1)] = jnp.concatenate(
            [low[:, :32], high[:, :32], low[:, 32:], high[:, 32:]], axis=1
        )


def regroup_back_to(out_ref, values):
    for k in range(16):
        tile = values[:, 128 * k : 128 * (k + 1)]
        out_ref[:, 64 * k : 64 * k + 64] = jnp.concatenate([tile[:, :32], tile[:, 64:96]], axis=1)
        out_ref[:, 1024 + 64 * k : 1088 + 64 * k] = jnp.concatenate([tile[:, 32:64], tile[:, 96:]], axis=1)


def regroup_kernel(in_ref, out_ref):
    regroup_to(out_ref, in_ref[...])


def regroup(values):
    return call(regroup_kernel, [values.shape], values)[0]


def to_other_core(rows):
    return shift(rows, "c", 1, 2)


def split_sum_kernel(own_ref, got_ref, kept_ref, *sent_refs):
    total = own_ref[...].astype(f32) + got_ref[...].astype(f32)
    rows = kept_ref.shape[0]
    kept_ref[...] = total[:rows]
    for at, sent_ref in enumerate(sent_refs):
        sent_ref[...] = total[rows * (at + 1) : rows * (at + 2)].astype(bf16)


def split_sum(own, got):
    rows, width = HALF, own.shape[1]
    return call(split_sum_kernel, [((rows, width), f32)] + [(rows, width)] * (own.shape[0] // rows - 1), own, got)


def group_gather(rows):
    own = (rows, *together(*(shift(rows, CHIP_X, -ahead, 4) for ahead in (1, 2, 3))))
    return [(block, to_other_core(block)) for block in own]


def line_sum(terms, axis):
    return jnp.sum(lax.all_to_all(terms, axis, 0, 0, tiled=True).astype(f32), axis=0)


def ring_sum(terms, axis, dim=0):
    place = lax.axis_index(axis)

    def term(ahead):
        return lax.dynamic_index_in_dim(terms, (place + ahead) % 4, dim, keepdims=False)

    return term(0).astype(f32) + sum(shift(term(ahead), axis, ahead, 4).astype(f32) for ahead in (1, 2, 3))


def head_rows(flip):
    pairs = []
    for a in range(2):
        for b in range(2):
            for z in range(4):
                for xl in range(2):
                    for c in range(2):
                        source = (((2 * a + b) * 4 + z) * 2 + xl) * 2 + c
                        to_y, to_z = 2 * b + z // 2, 2 * (z % 2) + xl
                        pairs.append((source, ((to_y * 4 + to_z) * 2 + (c ^ flip)) * 2 + a))
    return pairs


def back_rows(flip):
    return [(there, here) for here, there in head_rows(flip)]


FSDP = ("y", "z", "xl", "c")


def rms_scale(values):
    return lax.rsqrt(jnp.mean(values * values, axis=1, keepdims=True) + EPS)


def norm_back(grad_normed, normed, scale_rows, gain):
    scaled = grad_normed * gain
    return scale_rows * (scaled - normed * jnp.mean(scaled * normed, axis=1, keepdims=True))


def resid_kernel(tokens_ref, kept_ref, got_ref, gain_ref, resid_ref, xn_ref):
    resid = tokens_ref[...].astype(f32) + kept_ref[...] + got_ref[...].astype(f32)
    resid_ref[...] = resid
    xn_ref[...] = (resid * rms_scale(resid) * gain_ref[...]).astype(bf16)


def grad_resid_kernel(resid_ref, gain_ref, cot_ref, own_ref, other_ref, *refs):
    grad = own_ref[...].astype(f32) + other_ref[...].astype(f32) + sum(ref[...].astype(f32) for ref in refs[:3])
    resid = resid_ref[...]
    scale = rms_scale(resid)
    grad = cot_ref[...].astype(f32) + norm_back(grad, resid * scale, scale, gain_ref[...])
    refs[3][...] = grad
    refs[4][...] = grad.astype(bf16)


def input_grad_kernel(tokens_ref, gain_ref, grad_resid_ref, kept_ref, got_ref, out_ref):
    inputs = tokens_ref[...].astype(f32)
    scale = rms_scale(inputs)
    grad = kept_ref[...] + got_ref[...].astype(f32)
    regroup_back_to(out_ref, grad_resid_ref[...] + norm_back(grad, inputs * scale, scale, gain_ref[...]))


def block_output_kernel(resid_ref, kept_ref, *refs):
    out = resid_ref[...] + kept_ref[...] + sum(ref[...].astype(f32) for ref in refs[:3])
    regroup_back_to(refs[3], out.astype(bf16))


def out_grad_kernel(kept_ref, given_ref, out_ref):
    regroup_back_to(out_ref, kept_ref[...].astype(f32) + given_ref[...].astype(f32))


def rotate_half(values):
    width = values.shape[1]
    lane = lax.broadcasted_iota(jnp.int32, values.shape, 1) % HEAD_DIM
    later = pltpu.roll(values, width - HEAD_DIM // 2, 1)
    earlier = pltpu.roll(values, HEAD_DIM // 2, 1)
    return jnp.where(lane < HEAD_DIM // 2, -later, earlier)


def head(values, h):
    return values[:, HEAD_DIM * h : HEAD_DIM * (h + 1)]


def allowed_places(first):
    shape = (LENGTH, LENGTH)
    rows = (lax.broadcasted_iota(jnp.int32, shape, 0) + first) & (LENGTH - 1)
    return ((lax.broadcasted_iota(jnp.int32, shape, 1) + first) & (LENGTH - 1)) <= rows


def probabilities(query, key, allowed):
    scores = jnp.where(allowed, contract(query, key, 1, 1) * HEAD_DIM**-0.5, NEG)
    exp_scores = jnp.exp(scores - jnp.max(scores, axis=1, keepdims=True))
    return exp_scores / jnp.sum(exp_scores, axis=1, keepdims=True)


def wide_table(ref, first, width):
    rows = ref[pl.ds(pl.multiple_of(first, HALF), LENGTH), :]
    return jnp.concatenate([rows] * (width // 128), axis=1)


def out_weights(full_ref):
    for j in range(4):
        width = min(640, 2048 - 640 * j)
        yield full_ref[:, 128 + 32 * j : 160 + 32 * j, :width].reshape(512, width), 640 * j, width


def gain_row(full_ref, which):
    at = 128 * (which + 1)
    return jnp.concatenate([full_ref[y, 224:240, at : at + 128].astype(f32)[:1] for y in range(16)], axis=1)


def gains_kernel(full_ref, *out_refs):
    for which, out_ref in enumerate(out_refs):
        out_ref[...] = gain_row(full_ref, which)


def attend_kernel(first_ref, own_ref, there_ref, full_ref, cos_ref, sin_ref, xn_ref, qkv_ref, mixed_ref, out_ref):
    first = first_ref[0]
    cosine, sine = wide_table(cos_ref, first, 512), wide_table(sin_ref, first, 512)
    inputs = jnp.concatenate([own_ref[...], there_ref[...]], axis=0).astype(f32)
    xn_ref[...] = (inputs * rms_scale(inputs) * gain_row(full_ref, 0)).astype(bf16)
    proj = contract(xn_ref[...], full_ref[:, :128, :].reshape(2048, 640), 1, 0).astype(bf16)
    query = proj[:, :512].astype(f32)
    query = (query * cosine + rotate_half(query) * sine).astype(bf16)
    qkv_ref[:, :512] = query
    wide = proj[:, 512:].astype(f32)
    turned = wide * cosine[:, :128] + rotate_half(wide) * sine[:, :128]
    lane = lax.broadcasted_iota(jnp.int32, wide.shape, 1)
    key_value = jnp.where(lane < HEAD_DIM, turned, wide).astype(bf16)
    qkv_ref[:, 512:] = key_value
    key, value = key_value[:, :HEAD_DIM], key_value[:, HEAD_DIM:]
    allowed = allowed_places(first)
    mixed = [
        contract(probabilities(head(query, h), key, allowed).astype(bf16), value, 1, 0) for h in range(8)
    ]
    mixed_ref[...] = jnp.concatenate(mixed, axis=1).astype(bf16)
    for weights, at, width in out_weights(full_ref):
        out_ref[:, at : at + width] = contract(mixed_ref[...], weights, 1, 0).astype(bf16)


def attend_back_kernel(first_ref, own_ref, there_ref, full_ref, cos_ref, sin_ref, qkv_ref, out_ref, back_ref):
    first = first_ref[0]
    cosine, sine = wide_table(cos_ref, first, 512), wide_table(sin_ref, first, 512)
    grad = jnp.concatenate([own_ref[...], there_ref[...]], axis=0)
    grad = sum(contract(grad[:, at : at + width], weights, 1, 1) for weights, at, width in out_weights(full_ref))
    grad = grad.astype(bf16)
    query = qkv_ref[:, :512]
    key_value = qkv_ref[:, 512:]
    key, value = key_value[:, :HEAD_DIM], key_value[:, HEAD_DIM:]
    allowed = allowed_places(first)
    grad_key = jnp.zeros((LENGTH, HEAD_DIM), f32)
    grad_value = jnp.zeros((LENGTH, HEAD_DIM), f32)
    grad_query = []
    for h in range(8):
        probs = probabilities(head(query, h), key, allowed)
        grad_probs = contract(head(grad, h), value, 1, 1)
        delta = jnp.sum(probs * grad_probs, axis=1, keepdims=True)
        grad_scores = (probs * (grad_probs - delta)).astype(bf16)
        grad_query.append(contract(grad_scores, key, 1, 0))
        grad_key = grad_key + contract(grad_scores, head(query, h), 0, 0)
        grad_value = grad_value + contract(probs.astype(bf16), head(grad, h), 0, 0)
    grad_query = jnp.concatenate(grad_query, axis=1) * HEAD_DIM**-0.5
    out_ref[:, :512] = (grad_query * cosine - rotate_half(grad_query * sine)).astype(bf16)
    wide = jnp.concatenate([grad_key * HEAD_DIM**-0.5, grad_value], axis=1)
    turned = wide * cosine[:, :128] - rotate_half(wide * sine[:, :128])
    lane = lax.broadcasted_iota(jnp.int32, wide.shape, 1)
    out_ref[:, 512:] = jnp.where(lane < HEAD_DIM, turned, wide).astype(bf16)
    back_ref[...] = contract(out_ref[...], full_ref[:, :128, :].reshape(2048, 640), 1, 1).astype(bf16)


def call(kernel, outs, *arrays, grid=(), in_specs=None, out_specs=None, hbm=False, held=(), flops=1 << 20):
    kind = pltpu.HBM if hbm else jax.ShapeDtypeStruct
    outs = [out if isinstance(out[1], type) or hasattr(out[1], "dtype") else (out, bf16) for out in outs]
    vmem, smem, block = pl.BlockSpec(memory_space=pltpu.VMEM), pl.BlockSpec(memory_space=pltpu.SMEM), pl.BlockSpec()
    if in_specs is None:
        in_specs = [smem if a.dtype == jnp.int32 else vmem if at in held else block for at, a in enumerate(arrays)]
    return pl.pallas_call(
        kernel,
        out_shape=[kind(shape, dtype) for shape, dtype in outs],
        grid=grid,
        in_specs=in_specs,
        out_specs=out_specs or [block] * len(outs),
        compiler_params=pltpu.CompilerParams(vmem_limit_bytes=20 * MIB),
        cost_estimate=pl.CostEstimate(flops=flops, bytes_accessed=1024, transcendentals=0),
    )(*arrays)


def mlp_kernel(part, own_ref, other_ref, own_cot_ref, other_cot_ref, w_ref, hidden_ref, grad_ref, back_ref, back_other_ref):
    xn = jnp.concatenate([own_ref[...], other_ref[...]], axis=0)
    cot = jnp.concatenate([own_cot_ref[...], other_cot_ref[...]], axis=0)
    wide = contract(xn, w_ref[:, : 2 * part], 1, 0)
    grad_hidden = contract(cot, w_ref[:, 2 * part :], 1, 0)
    gate, up = wide[:, :part], wide[:, part:]
    sigmoid_gate = jax.nn.sigmoid(gate)
    silu_gate = gate * sigmoid_gate
    hidden_ref[...] = (silu_gate * up).astype(bf16)
    grad_ref[:, :part] = (
        grad_hidden * up * (sigmoid_gate * (1.0 + gate * (1.0 - sigmoid_gate)))
    ).astype(bf16)
    grad_ref[:, part:] = (grad_hidden * silu_gate).astype(bf16)
    back = contract(grad_ref[...], w_ref[:, : 2 * part], 1, 1).astype(bf16)
    rows = own_ref.shape[0]
    back_ref[...] = back[:rows]
    back_other_ref[...] = back[rows:]


def mlp_out_kernel(part, *refs):
    hidden_refs, w_ref, out_refs = refs[:4], refs[4], refs[5:]
    for chip in range(4):
        out = contract(hidden_refs[chip][...], w_ref[:, 2 * part :], 1, 1).astype(bf16)
        rows = out.shape[0] // 2
        for core in range(2):
            out_refs[core][rows * chip : rows * (chip + 1), :] = out[rows * core : rows * (core + 1)]


def mlp_terms_kernel(part, *refs):
    xn, cot, grad, hidden = [
        jnp.concatenate([ref[...] for ref in group], axis=0) for group in (refs[:8], refs[8:16], refs[16:20], refs[20:24])
    ]
    out_ref = refs[24]
    out_ref[:, : 2 * part] = contract(xn, grad, 0, 0).astype(bf16)
    out_ref[:, 2 * part :] = contract(cot, hidden, 0, 0).astype(bf16)


def columns_spec(rows, block):
    return pl.BlockSpec((rows, block), lambda i: (0, i))


def whole_spec(array):
    return pl.BlockSpec(array.shape, lambda i: (0, 0), pipeline_mode=pl.Buffered(1))


def mlp_terms(part, xn, cot, grad, hidden):
    rows, width = xn[0].shape
    block = 256
    return call(
        functools.partial(mlp_terms_kernel, part),
        [(width, 3 * part)],
        *xn,
        *cot,
        *grad,
        *hidden,
        grid=(width // block,),
        in_specs=[columns_spec(rows, block)] * 16 + [whole_spec(a) for a in grad + hidden],
        out_specs=[pl.BlockSpec((block, 3 * part), lambda i: (i, 0))],
        hbm=True,
    )[0]


def out_terms_kernel(mixed_ref, mixed_other_ref, *refs):
    own, other = [jnp.concatenate([ref[...] for ref in pair], axis=0) for pair in (refs[:2], refs[2:4])]
    refs[4][...] = (contract(mixed_ref[...], own, 0, 0) + contract(mixed_other_ref[...], other, 0, 0)).astype(bf16)


def out_terms(mixed, grad):
    rows, width = grad[0][0].shape
    block = 512
    blocks = [columns_spec(rows, block)] * 4
    return call(
        out_terms_kernel,
        [(512, width)],
        *mixed,
        *grad[0],
        *grad[1],
        grid=(width // block,),
        in_specs=[whole_spec(a) for a in mixed] + blocks,
        out_specs=[columns_spec(512, block)],
        hbm=True,
    )[0]


def qkv_terms_kernel(xn_ref, xn_other_ref, grad_ref, grad_other_ref, out_ref):
    out_ref[...] = (
        contract(xn_ref[...], grad_ref[...], 0, 0) + contract(xn_other_ref[...], grad_other_ref[...], 0, 0)
    ).astype(bf16)


def qkv_terms(xn, grad):
    rows, width = xn[0].shape
    block = 512
    return call(
        qkv_terms_kernel,
        [(width, 640)],
        *xn,
        *grad,
        grid=(width // block,),
        in_specs=[columns_spec(rows, block)] * 2 + [whole_spec(a) for a in grad],
        out_specs=[pl.BlockSpec((block, 640), lambda i: (i, 0))],
        hbm=True,
    )[0]


def to_owners(share):
    return lax.all_to_all(share.reshape(MEMBERS, -1, share.shape[-1]), GROUP, 0, 0, tiled=True)


def line_terms_kernel(place_ref, in_ref, out_ref):
    for ahead in range(4):
        at = (place_ref[0] + ahead) % 4
        out_ref[ahead] = sum(in_ref[y, at].astype(f32) for y in range(4)).astype(bf16)


def line_terms(gathered, place):
    out = call(line_terms_kernel, [gathered.shape[1:]], place.astype(jnp.int32)[None], gathered)[0]
    return [out[ahead] for ahead in range(4)]


def shifted(terms, axis):
    return [shift(terms[ahead], axis, ahead, 4) for ahead in (1, 2, 3)]


def sum_kernel(*refs):
    refs[-1][...] = sum(ref[...].astype(f32) for ref in refs[:-1]).astype(bf16)


def unpack_kernel(part, in_ref, gate_ref, up_ref, down_ref, query_ref, key_ref, value_ref):
    for member in range(MEMBERS):
        for place, out_ref in enumerate((gate_ref, up_ref, down_ref)):
            at = 640 + part * place
            out_ref[:, part * member : part * (member + 1)] = in_ref[member, :, at : at + part].astype(f32)
    for own in range(4):
        total = in_ref[own, :, :640].astype(f32) + in_ref[own + 4, :, :640].astype(f32)
        query_ref[:, 512 * own : 512 * (own + 1)] = total[:, :512]
        key_ref[:, HEAD_DIM * own : HEAD_DIM * (own + 1)] = total[:, 512 : 512 + HEAD_DIM]
        value_ref[:, HEAD_DIM * own : HEAD_DIM * (own + 1)] = total[:, 512 + HEAD_DIM :]


def attn_pack_kernel(query_ref, key_ref, value_ref, gains_ref, out_ref):
    for member in range(MEMBERS):
        own = member % 4
        out_ref[member, :, :512] = query_ref[:, 512 * own : 512 * (own + 1)]
        out_ref[member, :, 512:640] = jnp.concatenate([head(key_ref, own), head(value_ref, own)], axis=1)
        out_ref[member, :, 640:768] = gains_ref[...]


def mlp_pack_kernel(part, gate_ref, up_ref, down_ref, out_ref):
    for member in range(MEMBERS):
        for place, ref in enumerate((gate_ref, up_ref, down_ref)):
            out_ref[member, :, part * place : part * (place + 1)] = ref[:, part * member : part * (member + 1)]


def rotary_tables():
    half = HEAD_DIM // 2
    frequency = 10000.0 ** (-2.0 * np.arange(half) / HEAD_DIM)
    places = np.arange(LENGTH + HALF) % LENGTH
    angles = np.tile(places[:, None] * frequency[None, :], (1, 4))
    return np.cos(angles).astype(np.float32), np.sin(angles).astype(np.float32)


def on_device(
    tokens, gain_attn, w_query, w_key, w_value, w_out, gain_mlp, w_gate, w_up, w_down, cotangent
):
    own_rows = w_query.shape[0]
    part = w_gate.shape[1] // MEMBERS

    gains = jnp.pad(jnp.concatenate([gain_attn, gain_mlp])[None, :], ((0, own_rows - 1), (0, 128 - 2 * own_rows)))
    block = call(attn_pack_kernel, [(MEMBERS, own_rows, 768)], w_query, w_key, w_value, gains)[0]
    out_block = regroup(w_out)
    block, here, there = together(
        lax.all_to_all(block, GROUP, 0, 0, tiled=True),
        lax.ppermute(out_block, FSDP, head_rows(0)),
        lax.ppermute(out_block, FSDP, head_rows(1)),
    )
    left = lax.axis_index("xl") == 0
    out_block = jnp.concatenate([jnp.where(left, here, there), jnp.where(left, there, here)], axis=0)
    gains = block[:, 0, 640 : 640 + 2 * own_rows].reshape(MEMBERS, 2, own_rows).swapaxes(0, 1).reshape(1, 256)
    gains = jnp.pad(gains, ((0, 2 * own_rows - 1), (0, 256)))
    attn_block = jnp.concatenate(
        [block[:, :, :640].reshape(MEMBERS * own_rows, 640)]
        + [out_block[:, 640 * j : 640 * (j + 1)] for j in range(3)]
        + [jnp.concatenate([out_block[:, 1920:], gains], axis=1)],
        axis=0,
    )
    mlp_block = call(functools.partial(mlp_pack_kernel, part), [(MEMBERS, own_rows, 3 * part)], w_gate, w_up, w_down)[0]
    mlp_block, attn_block = together(mlp_block, attn_block)
    attn_full = lax.all_gather(attn_block, PLANE, axis=0)
    own_tokens, own_cotangent = regroup(tokens[0]), regroup(cotangent[0])
    mlp_block, there_tokens, own_cotangent = together(
        lax.all_to_all(mlp_block, GROUP, 0, 0, tiled=True), shift(own_tokens, "xh", 1, 2), own_cotangent
    )
    mlp_block = mlp_block.reshape(MEMBERS * own_rows, 3 * part)
    mlp_w = lax.all_gather(mlp_block, PLANE, axis=0, tiled=True)

    pair_tokens = (own_tokens, there_tokens), (to_other_core(own_tokens), to_other_core(there_tokens))
    attn_full, pair_tokens, group_cotangent = together(attn_full, pair_tokens, group_gather(own_cotangent))
    gain_one, gain_two = call(gains_kernel, [((1, 2048), f32)] * 2, attn_full, held=(0,))

    first = (HALF * lax.axis_index("xh")).astype(jnp.int32)[None]
    cosine, sine = rotary_tables()

    def attend(chunks):
        shapes = [(LENGTH, 2048), (LENGTH, 640), (LENGTH, 512), (LENGTH, 2048)]
        return call(attend_kernel, shapes, first, *chunks, attn_full, cosine, sine, held=(3,))

    xn_other, qkv_other, mixed_other, out_other = attend(pair_tokens[1])
    xn_own, qkv_own, mixed_own, out_own = attend(pair_tokens[0])
    kept, sent = split_sum(out_own, to_other_core(out_other))
    resid, xn_rows = call(
        resid_kernel, [((HALF, 2048), f32), (HALF, 2048)], own_tokens, kept, shift(sent, "xh", 1, 2), gain_two
    )

    def feed_forward(chip):
        shapes = [(LENGTH, part), (LENGTH, 2 * part), (HALF, 2048), (HALF, 2048)]
        return call(functools.partial(mlp_kernel, part), shapes, *xn_two[chip], *group_cotangent[chip], mlp_w, held=(4,), flops=M_FLOPS)

    arrived = together(*(shift(xn_rows, CHIP_X, -ahead, 4) for ahead in (1, 2, 3)))
    xn_two = [(rows, to_other_core(rows)) for rows in (xn_rows, *arrived)]
    results, got = [None] * 4, [None] * 4

    def core_total(ahead):
        return (results[ahead][2].astype(f32) + to_other_core(results[ahead][3]).astype(f32)).astype(bf16)

    results[2] = feed_forward(2)
    results[3] = feed_forward(3)
    far, xn_one_ahead = together(core_total(2), xn_two[1][0])
    xn_two[1] = xn_one_ahead, xn_two[1][1]
    results[1] = feed_forward(1)
    near, xn_own_rows = together(core_total(3), xn_rows)
    xn_two[0] = xn_own_rows, xn_two[0][1]
    got[3] = shift(near, CHIP_X, 3, 4)
    results[0], got[2] = together(feed_forward(0), shift(far, CHIP_X, 2, 4))
    got[1] = shift(core_total(1), CHIP_X, 1, 4)
    hidden, grad_wide, backs, back_others = (list(kind) for kind in zip(*results))
    flat = [[block for pair in pairs for block in pair] for pairs in (xn_two, group_cotangent)]
    own_other, got[1], got[3], mlp_term = together(
        to_other_core(back_others[0]), got[1], got[3], mlp_terms(part, *flat, grad_wide, hidden)
    )
    shares = lax.psum_scatter(mlp_term, PLANE, scatter_dimension=0, tiled=True)
    grad_resid, grad_rows = call(
        grad_resid_kernel,
        [((HALF, 2048), f32), (HALF, 2048)],
        *(resid, gain_two, own_cotangent, backs[0], own_other, *got[1:]),
    )
    grad_rows, hidden[0] = together(grad_rows, hidden[0])
    out_own, out_other = call(functools.partial(mlp_out_kernel, part), [(4 * HALF, 2048)] * 2, *hidden, mlp_w, held=(4,))
    grad_there, grad_rows_other, out_own, out_other = together(
        shift(grad_rows, "xh", 1, 2), to_other_core(grad_rows), out_own, out_other
    )
    grad_attn = (grad_rows, grad_there), (grad_rows_other, to_other_core(grad_there))

    def attend_back(chunks, qkv):
        shapes = [(LENGTH, 640), (LENGTH, 2048)]
        return call(attend_back_kernel, shapes, first, *chunks, attn_full, cosine, sine, qkv, held=(3,))

    (grad_own, back_own), other_chunks = together(attend_back(grad_attn[0], qkv_own), grad_attn[1])
    grad_other, back_other = attend_back(other_chunks, qkv_other)
    attn_term = qkv_terms((xn_own, xn_other), (grad_own, grad_other)).reshape(4, 4, 8 * own_rows, 640)
    attn_term, back_own, grad_attn, out_own = together(attn_term, back_own, grad_attn, out_own)
    kept, sent = split_sum(back_own, to_other_core(back_other))
    out_kept, *out_sent = split_sum(out_own, to_other_core(out_other))
    out_term = out_terms((mixed_own, mixed_other), grad_attn).reshape(4, 4, 2 * own_rows, 2048)
    attn_line, out_share, far_got, *near_got = together(
        lax.all_to_all(attn_term, "y", 0, 0, tiled=True),
        ring_sum(out_term, "z", 1).astype(bf16),
        shift(jnp.concatenate([sent, out_sent[1]], axis=0), CHIP_X, 2, 4),
        shift(out_sent[0], CHIP_X, 1, 4),
        shift(out_sent[2], CHIP_X, 3, 4),
    )
    attn_terms, out_share = together(line_terms(attn_line, lax.axis_index("z")), out_share)
    attn_share = call(sum_kernel, [(8 * own_rows, 640)], attn_terms[0], *shifted(attn_terms, "z"))[0]
    shares = jnp.concatenate([attn_share, shares], axis=1)
    shares, out_share = together(to_owners(shares), ring_sum(out_share, "y").astype(bf16))
    block_output = call(block_output_kernel, [(HALF, 2048)], resid, out_kept, *near_got, far_got[HALF:])[0]
    input_grad = call(input_grad_kernel, [((HALF, 2048), f32)], own_tokens, gain_one, grad_resid, kept, far_got[:HALF])[0]
    taken = jnp.where(left, out_share[:own_rows], out_share[own_rows:])
    given = jnp.where(left, out_share[own_rows:], out_share[:own_rows])
    taken = lax.ppermute(taken, FSDP, back_rows(0))
    given = lax.ppermute(given, FSDP, back_rows(1))
    gate_grad, up_grad, down_grad, query_grad, key_grad, value_grad = call(
        functools.partial(unpack_kernel, part),
        [((own_rows, MEMBERS * part), f32)] * 3
        + [((own_rows, 2048), f32), ((own_rows, 256), f32), ((own_rows, 256), f32)],
        shares,
    )
    out_grad = call(out_grad_kernel, [((own_rows, 2048), f32)], taken, given)[0]

    def gain_grad(gain, *pairs):
        total = sum(jnp.sum(w.astype(f32) * grad, axis=1) for w, grad in pairs)
        return total / gain.astype(f32)

    gain_attn_grad = gain_grad(gain_attn, (w_query, query_grad), (w_key, key_grad), (w_value, value_grad))
    gain_mlp_grad = gain_grad(gain_mlp, (w_gate, gate_grad), (w_up, up_grad))
    return (
        block_output[None],
        input_grad[None],
        gain_attn_grad,
        query_grad,
        key_grad,
        value_grad,
        out_grad,
        gain_mlp_grad,
        gate_grad,
        up_grad,
        down_grad,
    )


def solution(mesh):
    view = Mesh(mesh.devices.reshape(SIZES), AXES)
    split = P(("xh",) + FSDP)
    rows = P(("xh",) + FSDP, None)
    data = P(FSDP, "xh", None)
    return jax.shard_map(
        on_device,
        mesh=view,
        in_specs=(data, split, rows, rows, rows, rows, split, rows, rows, rows, data),
        out_specs=(data, data, split, rows, rows, rows, rows, split, rows, rows, rows),
        check_vma=False,
    )
```

```python
import functools

import jax
import jax.numpy as jnp
import numpy as np
from jax import lax
from jax.experimental import pallas as pl
from jax.experimental.pallas import tpu as pltpu
from jax.sharding import Mesh, PartitionSpec as P

HEADS = 32
KV_HEADS = 4
HEAD_DIM = 64
EPS = 1e-05
NEG = -1e30
LENGTH = 256
HALF = 128
MIB = 1024 * 1024
M_FLOPS = 1 << 20

AXES = ("xh", "y", "z", "xl", "c")
SIZES = (2, 4, 4, 2, 2)
CHIP_X = ("xh", "xl")
GROUP = ("xl", "xh", "c")
MEMBERS = 8
PAIRED = ("xh", "c")
PLANE = ("y", "z")

bf16 = jnp.bfloat16
f32 = jnp.float32


def contract(a, b, dim_a, dim_b):
    return lax.dot_general(a, b, (((dim_a,), (dim_b,)), ((), ())), preferred_element_type=f32)


def shift(values, axis, by, size):
    return lax.ppermute(values, axis, [(i, (i + by) % size) for i in range(size)])


def together(*values):
    return lax.optimization_barrier(values)


def regroup_to(out_ref, values):
    for k in range(16):
        low = values[:, 64 * k : 64 * k + 64]
        high = values[:, 1024 + 64 * k : 1088 + 64 * k]
        out_ref[:, 128 * k : 128 * (k + 1)] = jnp.concatenate(
            [low[:, :32], high[:, :32], low[:, 32:], high[:, 32:]], axis=1
        )


def regroup_back_to(out_ref, values):
    for k in range(16):
        tile = values[:, 128 * k : 128 * (k + 1)]
        out_ref[:, 64 * k : 64 * k + 64] = jnp.concatenate([tile[:, :32], tile[:, 64:96]], axis=1)
        out_ref[:, 1024 + 64 * k : 1088 + 64 * k] = jnp.concatenate([tile[:, 32:64], tile[:, 96:]], axis=1)


def regroup_kernel(in_ref, out_ref):
    regroup_to(out_ref, in_ref[...])


def regroup(values):
    return call(regroup_kernel, [values.shape], values)[0]


def to_other_core(rows):
    return shift(rows, "c", 1, 2)


def split_sum_kernel(own_ref, got_ref, kept_ref, *sent_refs):
    total = own_ref[...].astype(f32) + got_ref[...].astype(f32)
    rows = kept_ref.shape[0]
    kept_ref[...] = total[:rows]
    for at, sent_ref in enumerate(sent_refs):
        sent_ref[...] = total[rows * (at + 1) : rows * (at + 2)].astype(bf16)


def split_sum(own, got):
    rows, width = HALF, own.shape[1]
    return call(split_sum_kernel, [((rows, width), f32)] + [(rows, width)] * (own.shape[0] // rows - 1), own, got)


def group_gather(rows):
    own = (rows, *together(*(shift(rows, CHIP_X, -ahead, 4) for ahead in (1, 2, 3))))
    return [(block, to_other_core(block)) for block in own]


def line_sum(terms, axis):
    return jnp.sum(lax.all_to_all(terms, axis, 0, 0, tiled=True).astype(f32), axis=0)


def head_rows(flip):
    pairs = []
    for a in range(2):
        for b in range(2):
            for z in range(4):
                for xl in range(2):
                    for c in range(2):
                        source = (((2 * a + b) * 4 + z) * 2 + xl) * 2 + c
                        to_y, to_z = 2 * b + z // 2, 2 * (z % 2) + xl
                        pairs.append((source, ((to_y * 4 + to_z) * 2 + (c ^ flip)) * 2 + a))
    return pairs


def back_rows(flip):
    return [(there, here) for here, there in head_rows(flip)]


FSDP = ("y", "z", "xl", "c")


def rms_scale(values):
    return lax.rsqrt(jnp.mean(values * values, axis=1, keepdims=True) + EPS)


def norm_back(grad_normed, normed, scale_rows, gain):
    scaled = grad_normed * gain
    return scale_rows * (scaled - normed * jnp.mean(scaled * normed, axis=1, keepdims=True))


def resid_kernel(tokens_ref, kept_ref, got_ref, gain_ref, resid_ref, xn_ref):
    resid = tokens_ref[...].astype(f32) + kept_ref[...] + got_ref[...].astype(f32)
    resid_ref[...] = resid
    xn_ref[...] = (resid * rms_scale(resid) * gain_ref[...]).astype(bf16)


def grad_resid_kernel(resid_ref, gain_ref, cot_ref, own_ref, other_ref, *refs):
    grad = own_ref[...].astype(f32) + other_ref[...].astype(f32) + sum(ref[...].astype(f32) for ref in refs[:3])
    resid = resid_ref[...]
    scale = rms_scale(resid)
    grad = cot_ref[...].astype(f32) + norm_back(grad, resid * scale, scale, gain_ref[...])
    refs[3][...] = grad
    refs[4][...] = grad.astype(bf16)


def input_grad_kernel(tokens_ref, gain_ref, grad_resid_ref, kept_ref, got_ref, out_ref):
    inputs = tokens_ref[...].astype(f32)
    scale = rms_scale(inputs)
    grad = kept_ref[...] + got_ref[...].astype(f32)
    regroup_back_to(out_ref, grad_resid_ref[...] + norm_back(grad, inputs * scale, scale, gain_ref[...]))


def block_output_kernel(resid_ref, kept_ref, *refs):
    out = resid_ref[...] + kept_ref[...] + sum(ref[...].astype(f32) for ref in refs[:3])
    regroup_back_to(refs[3], out.astype(bf16))


def out_grad_kernel(kept_ref, given_ref, out_ref):
    regroup_back_to(out_ref, kept_ref[...].astype(f32) + given_ref[...].astype(f32))


def rotate_half(values):
    width = values.shape[1]
    lane = lax.broadcasted_iota(jnp.int32, values.shape, 1) % HEAD_DIM
    later = pltpu.roll(values, width - HEAD_DIM // 2, 1)
    earlier = pltpu.roll(values, HEAD_DIM // 2, 1)
    return jnp.where(lane < HEAD_DIM // 2, -later, earlier)


def head(values, h):
    return values[:, HEAD_DIM * h : HEAD_DIM * (h + 1)]


def allowed_places(first):
    shape = (LENGTH, LENGTH)
    rows = (lax.broadcasted_iota(jnp.int32, shape, 0) + first) & (LENGTH - 1)
    return ((lax.broadcasted_iota(jnp.int32, shape, 1) + first) & (LENGTH - 1)) <= rows


def probabilities(query, key, allowed):
    scores = jnp.where(allowed, contract(query, key, 1, 1) * HEAD_DIM**-0.5, NEG)
    exp_scores = jnp.exp(scores - jnp.max(scores, axis=1, keepdims=True))
    return exp_scores / jnp.sum(exp_scores, axis=1, keepdims=True)


def wide_table(ref, first, width):
    rows = ref[pl.ds(pl.multiple_of(first, HALF), LENGTH), :]
    return jnp.concatenate([rows] * (width // 128), axis=1)


def out_weights(full_ref):
    for j in range(4):
        width = min(640, 2048 - 640 * j)
        yield full_ref[:, 128 + 32 * j : 160 + 32 * j, :width].reshape(512, width), 640 * j, width


def gain_row(full_ref, which):
    at = 128 * (which + 1)
    return jnp.concatenate([full_ref[y, 224:240, at : at + 128].astype(f32)[:1] for y in range(16)], axis=1)


def gains_kernel(full_ref, *out_refs):
    for which, out_ref in enumerate(out_refs):
        out_ref[...] = gain_row(full_ref, which)


def attend_kernel(first_ref, own_ref, there_ref, full_ref, cos_ref, sin_ref, xn_ref, qkv_ref, mixed_ref, out_ref):
    first = first_ref[0]
    cosine, sine = wide_table(cos_ref, first, 512), wide_table(sin_ref, first, 512)
    inputs = jnp.concatenate([own_ref[...], there_ref[...]], axis=0).astype(f32)
    xn_ref[...] = (inputs * rms_scale(inputs) * gain_row(full_ref, 0)).astype(bf16)
    proj = contract(xn_ref[...], full_ref[:, :128, :].reshape(2048, 640), 1, 0).astype(bf16)
    query = proj[:, :512].astype(f32)
    query = (query * cosine + rotate_half(query) * sine).astype(bf16)
    qkv_ref[:, :512] = query
    wide = proj[:, 512:].astype(f32)
    turned = wide * cosine[:, :128] + rotate_half(wide) * sine[:, :128]
    lane = lax.broadcasted_iota(jnp.int32, wide.shape, 1)
    key_value = jnp.where(lane < HEAD_DIM, turned, wide).astype(bf16)
    qkv_ref[:, 512:] = key_value
    key, value = key_value[:, :HEAD_DIM], key_value[:, HEAD_DIM:]
    allowed = allowed_places(first)
    mixed = [
        contract(probabilities(head(query, h), key, allowed).astype(bf16), value, 1, 0) for h in range(8)
    ]
    mixed_ref[...] = jnp.concatenate(mixed, axis=1).astype(bf16)
    for weights, at, width in out_weights(full_ref):
        out_ref[:, at : at + width] = contract(mixed_ref[...], weights, 1, 0).astype(bf16)


def attend_back_kernel(first_ref, own_ref, there_ref, full_ref, cos_ref, sin_ref, qkv_ref, out_ref, back_ref):
    first = first_ref[0]
    cosine, sine = wide_table(cos_ref, first, 512), wide_table(sin_ref, first, 512)
    grad = jnp.concatenate([own_ref[...], there_ref[...]], axis=0)
    grad = sum(contract(grad[:, at : at + width], weights, 1, 1) for weights, at, width in out_weights(full_ref))
    grad = grad.astype(bf16)
    query = qkv_ref[:, :512]
    key_value = qkv_ref[:, 512:]
    key, value = key_value[:, :HEAD_DIM], key_value[:, HEAD_DIM:]
    allowed = allowed_places(first)
    grad_key = jnp.zeros((LENGTH, HEAD_DIM), f32)
    grad_value = jnp.zeros((LENGTH, HEAD_DIM), f32)
    grad_query = []
    for h in range(8):
        probs = probabilities(head(query, h), key, allowed)
        grad_probs = contract(head(grad, h), value, 1, 1)
        delta = jnp.sum(probs * grad_probs, axis=1, keepdims=True)
        grad_scores = (probs * (grad_probs - delta)).astype(bf16)
        grad_query.append(contract(grad_scores, key, 1, 0))
        grad_key = grad_key + contract(grad_scores, head(query, h), 0, 0)
        grad_value = grad_value + contract(probs.astype(bf16), head(grad, h), 0, 0)
    grad_query = jnp.concatenate(grad_query, axis=1) * HEAD_DIM**-0.5
    out_ref[:, :512] = (grad_query * cosine - rotate_half(grad_query * sine)).astype(bf16)
    wide = jnp.concatenate([grad_key * HEAD_DIM**-0.5, grad_value], axis=1)
    turned = wide * cosine[:, :128] - rotate_half(wide * sine[:, :128])
    lane = lax.broadcasted_iota(jnp.int32, wide.shape, 1)
    out_ref[:, 512:] = jnp.where(lane < HEAD_DIM, turned, wide).astype(bf16)
    back_ref[...] = contract(out_ref[...], full_ref[:, :128, :].reshape(2048, 640), 1, 1).astype(bf16)


def call(kernel, outs, *arrays, grid=(), in_specs=None, out_specs=None, hbm=False, held=(), flops=1 << 20, scratch=(), vmem_mib=20):
    kind = pltpu.HBM if hbm else jax.ShapeDtypeStruct
    outs = [out if isinstance(out[1], type) or hasattr(out[1], "dtype") else (out, bf16) for out in outs]
    vmem, smem, block = pl.BlockSpec(memory_space=pltpu.VMEM), pl.BlockSpec(memory_space=pltpu.SMEM), pl.BlockSpec()
    if in_specs is None:
        in_specs = [smem if a.dtype == jnp.int32 else vmem if at in held else block for at, a in enumerate(arrays)]
    return pl.pallas_call(
        kernel,
        out_shape=[kind(shape, dtype) for shape, dtype in outs],
        grid=grid,
        in_specs=in_specs,
        out_specs=out_specs or [block] * len(outs),
        scratch_shapes=scratch,
        compiler_params=pltpu.CompilerParams(vmem_limit_bytes=vmem_mib * MIB),
        cost_estimate=pl.CostEstimate(flops=flops, bytes_accessed=1024, transcendentals=0),
    )(*arrays)


def mlp_kernel(part, own_ref, other_ref, own_cot_ref, other_cot_ref, w_ref, hidden_ref, grad_ref, back_ref, back_other_ref):
    xn = jnp.concatenate([own_ref[...], other_ref[...]], axis=0)
    cot = jnp.concatenate([own_cot_ref[...], other_cot_ref[...]], axis=0)
    wide = contract(xn, w_ref[:, : 2 * part], 1, 0)
    grad_hidden = contract(cot, w_ref[:, 2 * part :], 1, 0)
    gate, up = wide[:, :part], wide[:, part:]
    sigmoid_gate = jax.nn.sigmoid(gate)
    silu_gate = gate * sigmoid_gate
    hidden_ref[...] = (silu_gate * up).astype(bf16)
    grad_ref[:, :part] = (
        grad_hidden * up * (sigmoid_gate * (1.0 + gate * (1.0 - sigmoid_gate)))
    ).astype(bf16)
    grad_ref[:, part:] = (grad_hidden * silu_gate).astype(bf16)
    back = contract(grad_ref[...], w_ref[:, : 2 * part], 1, 1).astype(bf16)
    rows = own_ref.shape[0]
    back_ref[...] = back[:rows]
    back_other_ref[...] = back[rows:]


def mlp_out_kernel(part, *refs):
    hidden_refs, w_ref, out_refs = refs[:4], refs[4], refs[5:]
    for chip in range(4):
        out = contract(hidden_refs[chip][...], w_ref[:, 2 * part :], 1, 1).astype(bf16)
        rows = out.shape[0] // 2
        for core in range(2):
            out_refs[core][rows * chip : rows * (chip + 1), :] = out[rows * core : rows * (core + 1)]


def mlp_terms_kernel(part, *refs):
    xn, cot, grad, hidden = [
        jnp.concatenate([ref[...] for ref in group], axis=0) for group in (refs[:8], refs[8:16], refs[16:20], refs[20:24])
    ]
    out_ref = refs[24]
    out_ref[:, : 2 * part] = contract(xn, grad, 0, 0).astype(bf16)
    out_ref[:, 2 * part :] = contract(cot, hidden, 0, 0).astype(bf16)


def columns_spec(rows, block):
    return pl.BlockSpec((rows, block), lambda i: (0, i))


def whole_spec(array):
    return pl.BlockSpec(array.shape, lambda i: (0, 0), pipeline_mode=pl.Buffered(1))


def mlp_terms(part, xn, cot, grad, hidden):
    rows, width = xn[0].shape
    block = 512
    return call(
        functools.partial(mlp_terms_kernel, part),
        [(width, 3 * part)],
        *xn,
        *cot,
        *grad,
        *hidden,
        grid=(width // block,),
        in_specs=[columns_spec(rows, block)] * 16 + [whole_spec(a) for a in grad + hidden],
        out_specs=[pl.BlockSpec((block, 3 * part), lambda i: (i, 0))],
        hbm=True,
        vmem_mib=32,
    )[0]


def out_terms_kernel(place_ref, mixed_ref, mixed_other_ref, *refs):
    own, other = [jnp.concatenate([ref[...] for ref in pair], axis=0) for pair in (refs[:2], refs[2:4])]
    terms_ref, out_refs = refs[8], refs[4:8]
    terms_ref[...] = (contract(mixed_ref[...], own, 0, 0) + contract(mixed_other_ref[...], other, 0, 0)).astype(bf16)
    for ahead, out_ref in enumerate(out_refs):
        at = (place_ref[0] + ahead) % 4
        for y in range(4):
            out_ref[y] = terms_ref[pl.ds(pl.multiple_of((4 * y + at) * 32, 32), 32), :]


def out_terms(place, mixed, grad):
    rows, width = grad[0][0].shape
    block = 512
    blocks = [columns_spec(rows, block)] * 4
    return call(
        out_terms_kernel,
        [(4, 32, width)] * 4,
        place.astype(jnp.int32)[None],
        *mixed,
        *grad[0],
        *grad[1],
        grid=(width // block,),
        in_specs=[pl.BlockSpec(memory_space=pltpu.SMEM)] + [whole_spec(a) for a in mixed] + blocks,
        out_specs=[pl.BlockSpec((4, 32, block), lambda i: (0, 0, i))] * 4,
        scratch=[pltpu.VMEM((512, block), bf16)],
    )


def qkv_terms_kernel(xn_ref, xn_other_ref, grad_ref, grad_other_ref, out_ref):
    out_ref[...] = (
        contract(xn_ref[...], grad_ref[...], 0, 0) + contract(xn_other_ref[...], grad_other_ref[...], 0, 0)
    ).astype(bf16)


def qkv_terms(xn, grad):
    rows, width = xn[0].shape
    block = 1024
    return call(
        qkv_terms_kernel,
        [(width, 640)],
        *xn,
        *grad,
        grid=(width // block,),
        in_specs=[columns_spec(rows, block)] * 2 + [whole_spec(a) for a in grad],
        out_specs=[pl.BlockSpec((block, 640), lambda i: (i, 0))],
        hbm=True,
    )[0]


def line_terms_kernel(place_ref, in_ref, *out_refs):
    for ahead, out_ref in enumerate(out_refs):
        at = (place_ref[0] + ahead) % 4
        out_ref[...] = sum(in_ref[y, at].astype(f32) for y in range(4)).astype(bf16)


def line_terms(gathered, place):
    return call(line_terms_kernel, [gathered.shape[2:]] * 4, place.astype(jnp.int32)[None], gathered, flops=64 << 30)


def shifted(terms, axis):
    return [terms[0]] + [shift(terms[ahead], axis, ahead, 4) for ahead in (1, 2, 3)]


def sum_kernel(*refs):
    refs[-1][...] = sum(ref[...].astype(f32) for ref in refs[:-1]).astype(bf16)


def shares_kernel(mlp_ref, *refs):
    out_ref = refs[-1]
    total = sum(ref[...].astype(f32) for ref in refs[:-1]).astype(bf16)
    rows = out_ref.shape[1]
    for member in range(MEMBERS):
        out_ref[member, :, :640] = total[rows * member : rows * (member + 1)]
        out_ref[member, :, 640:] = mlp_ref[rows * member : rows * (member + 1), :]


def ring_terms_kernel(place_ref, *refs):
    for ahead, out_ref in enumerate(refs[4:]):
        at = (place_ref[0] + ahead) % 4
        out_ref[...] = sum(ref[at].astype(f32) for ref in refs[:4]).astype(bf16)


def unpack_kernel(part, in_ref, gate_ref, up_ref, down_ref, query_ref, key_ref, value_ref):
    for member in range(MEMBERS):
        for place, out_ref in enumerate((gate_ref, up_ref, down_ref)):
            at = 640 + part * place
            out_ref[:, part * member : part * (member + 1)] = in_ref[member, :, at : at + part].astype(f32)
    for own in range(4):
        total = in_ref[own, :, :640].astype(f32) + in_ref[own + 4, :, :640].astype(f32)
        query_ref[:, 512 * own : 512 * (own + 1)] = total[:, :512]
        key_ref[:, HEAD_DIM * own : HEAD_DIM * (own + 1)] = total[:, 512 : 512 + HEAD_DIM]
        value_ref[:, HEAD_DIM * own : HEAD_DIM * (own + 1)] = total[:, 512 + HEAD_DIM :]


def attn_pack_kernel(query_ref, key_ref, value_ref, gains_ref, out_ref):
    for member in range(MEMBERS):
        own = member % 4
        out_ref[member, :, :512] = query_ref[:, 512 * own : 512 * (own + 1)]
        out_ref[member, :, 512:640] = jnp.concatenate([head(key_ref, own), head(value_ref, own)], axis=1)
        out_ref[member, :, 640:768] = gains_ref[...]


def mlp_pack_kernel(part, gate_ref, up_ref, down_ref, out_ref):
    for member in range(MEMBERS):
        for place, ref in enumerate((gate_ref, up_ref, down_ref)):
            out_ref[member, :, part * place : part * (place + 1)] = ref[:, part * member : part * (member + 1)]


def rotary_tables():
    half = HEAD_DIM // 2
    frequency = 10000.0 ** (-2.0 * np.arange(half) / HEAD_DIM)
    places = np.arange(LENGTH + HALF) % LENGTH
    angles = np.tile(places[:, None] * frequency[None, :], (1, 4))
    return np.cos(angles).astype(np.float32), np.sin(angles).astype(np.float32)


def on_device(
    tokens, gain_attn, w_query, w_key, w_value, w_out, gain_mlp, w_gate, w_up, w_down, cotangent
):
    own_rows = w_query.shape[0]
    part = w_gate.shape[1] // MEMBERS

    gains = jnp.pad(jnp.concatenate([gain_attn, gain_mlp])[None, :], ((0, own_rows - 1), (0, 128 - 2 * own_rows)))
    block = call(attn_pack_kernel, [(MEMBERS, own_rows, 768)], w_query, w_key, w_value, gains)[0]
    out_block = regroup(w_out)
    block, here, there = together(
        lax.all_to_all(block, GROUP, 0, 0, tiled=True),
        lax.ppermute(out_block, FSDP, head_rows(0)),
        lax.ppermute(out_block, FSDP, head_rows(1)),
    )
    left = lax.axis_index("xl") == 0
    out_block = jnp.concatenate([jnp.where(left, here, there), jnp.where(left, there, here)], axis=0)
    gains = block[:, 0, 640 : 640 + 2 * own_rows].reshape(MEMBERS, 2, own_rows).swapaxes(0, 1).reshape(1, 256)
    gains = jnp.pad(gains, ((0, 2 * own_rows - 1), (0, 256)))
    attn_block = jnp.concatenate(
        [block[:, :, :640].reshape(MEMBERS * own_rows, 640)]
        + [out_block[:, 640 * j : 640 * (j + 1)] for j in range(3)]
        + [jnp.concatenate([out_block[:, 1920:], gains], axis=1)],
        axis=0,
    )
    mlp_block = call(functools.partial(mlp_pack_kernel, part), [(MEMBERS, own_rows, 3 * part)], w_gate, w_up, w_down)[0]
    mlp_block, attn_block = together(mlp_block, attn_block)
    attn_full = lax.all_gather(attn_block, PLANE, axis=0)
    own_tokens, own_cotangent = regroup(tokens[0]), regroup(cotangent[0])
    mlp_block, there_tokens, own_cotangent = together(
        lax.all_to_all(mlp_block, GROUP, 0, 0, tiled=True), shift(own_tokens, "xh", 1, 2), own_cotangent
    )
    mlp_block = mlp_block.reshape(MEMBERS * own_rows, 3 * part)
    mlp_w = lax.all_gather(mlp_block, PLANE, axis=0, tiled=True)

    pair_tokens = (own_tokens, there_tokens), (to_other_core(own_tokens), to_other_core(there_tokens))
    attn_full, pair_tokens, group_cotangent = together(attn_full, pair_tokens, group_gather(own_cotangent))
    gain_one, gain_two = call(gains_kernel, [((1, 2048), f32)] * 2, attn_full, held=(0,))

    first = (HALF * lax.axis_index("xh")).astype(jnp.int32)[None]
    cosine, sine = rotary_tables()

    def attend(chunks):
        shapes = [(LENGTH, 2048), (LENGTH, 640), (LENGTH, 512), (LENGTH, 2048)]
        return call(attend_kernel, shapes, first, *chunks, attn_full, cosine, sine, held=(3,))

    xn_other, qkv_other, mixed_other, out_other = attend(pair_tokens[1])
    xn_own, qkv_own, mixed_own, out_own = attend(pair_tokens[0])
    kept, sent = split_sum(out_own, to_other_core(out_other))
    resid, xn_rows = call(
        resid_kernel, [((HALF, 2048), f32), (HALF, 2048)], own_tokens, kept, shift(sent, "xh", 1, 2), gain_two
    )

    def feed_forward(chip):
        shapes = [(LENGTH, part), (LENGTH, 2 * part), (HALF, 2048), (HALF, 2048)]
        return call(functools.partial(mlp_kernel, part), shapes, *xn_two[chip], *group_cotangent[chip], mlp_w, held=(4,), flops=M_FLOPS)

    arrived = together(*(shift(xn_rows, CHIP_X, -ahead, 4) for ahead in (1, 2, 3)))
    xn_two = [(rows, to_other_core(rows)) for rows in (xn_rows, *arrived)]
    results, got = [None] * 4, [None] * 4

    def core_total(ahead):
        return (results[ahead][2].astype(f32) + to_other_core(results[ahead][3]).astype(f32)).astype(bf16)

    results[2] = feed_forward(2)
    results[3] = feed_forward(3)
    far, xn_one_ahead = together(core_total(2), xn_two[1][0])
    xn_two[1] = xn_one_ahead, xn_two[1][1]
    results[1] = feed_forward(1)
    near, xn_own_rows = together(core_total(3), xn_rows)
    xn_two[0] = xn_own_rows, xn_two[0][1]
    got[3] = shift(near, CHIP_X, 3, 4)
    results[0], got[2] = together(feed_forward(0), shift(far, CHIP_X, 2, 4))
    got[1] = shift(core_total(1), CHIP_X, 1, 4)
    hidden, grad_wide, backs, back_others = (list(kind) for kind in zip(*results))
    flat = [[block for pair in pairs for block in pair] for pairs in (xn_two, group_cotangent)]
    own_other, got[1], got[3], mlp_term = together(
        to_other_core(back_others[0]), got[1], got[3], mlp_terms(part, *flat, grad_wide, hidden)
    )
    shares = lax.psum_scatter(mlp_term, PLANE, scatter_dimension=0, tiled=True)
    grad_resid, grad_rows = call(
        grad_resid_kernel,
        [((HALF, 2048), f32), (HALF, 2048)],
        *(resid, gain_two, own_cotangent, backs[0], own_other, *got[1:]),
    )
    grad_rows, hidden[0] = together(grad_rows, hidden[0])
    out_own, out_other = call(functools.partial(mlp_out_kernel, part), [(4 * HALF, 2048)] * 2, *hidden, mlp_w)
    grad_there, grad_rows_other, out_own, out_other = together(
        shift(grad_rows, "xh", 1, 2), to_other_core(grad_rows), out_own, out_other
    )
    grad_attn = (grad_rows, grad_there), (grad_rows_other, to_other_core(grad_there))

    def attend_back(chunks, qkv):
        shapes = [(LENGTH, 640), (LENGTH, 2048)]
        return call(attend_back_kernel, shapes, first, *chunks, attn_full, cosine, sine, qkv, held=(3,))

    (grad_own, back_own), other_chunks, (out_kept, *out_sent) = together(
        attend_back(grad_attn[0], qkv_own), grad_attn[1], split_sum(out_own, to_other_core(out_other))
    )
    grad_other, back_other = attend_back(other_chunks, qkv_other)
    attn_term = qkv_terms((xn_own, xn_other), (grad_own, grad_other)).reshape(4, 4, 8 * own_rows, 640)
    attn_term, back_own, grad_attn = together(attn_term, back_own, grad_attn)
    kept, sent = split_sum(back_own, to_other_core(back_other))
    out_term = out_terms(lax.axis_index("z"), (mixed_own, mixed_other), grad_attn)
    out_got = [shift(rows, CHIP_X, ahead, 4) for ahead, rows in zip((1, 2, 3), out_sent)]
    grad_got = shift(sent, "xh", 1, 2)
    place_y = lax.axis_index("y").astype(jnp.int32)[None]
    attn_terms, out_term, out_got = together(
        line_terms(lax.all_to_all(attn_term, "y", 0, 0, tiled=True), lax.axis_index("z")),
        shifted(out_term, "z"),
        out_got,
    )
    shares = call(
        shares_kernel, [(MEMBERS, own_rows, 640 + 3 * part)], shares, *shifted(attn_terms, "z")
    )[0]
    shares, out_term, grad_got = together(shares, out_term, grad_got)
    out_term = call(ring_terms_kernel, [(2 * own_rows, 2048)] * 4, place_y, *out_term)
    out_share = call(sum_kernel, [(2 * own_rows, 2048)], *shifted(out_term, "y"))[0]
    block_output = call(block_output_kernel, [(HALF, 2048)], resid, out_kept, *out_got)[0]
    input_grad = call(input_grad_kernel, [((HALF, 2048), f32)], own_tokens, gain_one, grad_resid, kept, grad_got)[0]
    taken = jnp.where(left, out_share[:own_rows], out_share[own_rows:])
    given = jnp.where(left, out_share[own_rows:], out_share[:own_rows])
    taken = lax.ppermute(taken, FSDP, back_rows(0))
    given = lax.ppermute(given, FSDP, back_rows(1))
    shares, block_output, input_grad = together(
        call(
            functools.partial(unpack_kernel, part),
            [((own_rows, MEMBERS * part), f32)] * 3
            + [((own_rows, 2048), f32), ((own_rows, 256), f32), ((own_rows, 256), f32)],
            lax.all_to_all(shares, GROUP, 0, 0, tiled=True),
            flops=64 << 30,
        ),
        block_output,
        input_grad,
    )
    gate_grad, up_grad, down_grad, query_grad, key_grad, value_grad = shares
    def gain_grad(gain, *pairs):
        total = sum(jnp.sum(w.astype(f32) * grad, axis=1) for w, grad in pairs)
        return total / gain.astype(f32)

    gain_attn_grad = gain_grad(gain_attn, (w_query, query_grad), (w_key, key_grad), (w_value, value_grad))
    gain_mlp_grad = gain_grad(gain_mlp, (w_gate, gate_grad), (w_up, up_grad))
    gain_attn_grad, gain_mlp_grad, taken, given = together(gain_attn_grad, gain_mlp_grad, taken, given)
    out_grad = call(out_grad_kernel, [((own_rows, 2048), f32)], taken, given)[0]
    return (
        block_output[None],
        input_grad[None],
        gain_attn_grad,
        query_grad,
        key_grad,
        value_grad,
        out_grad,
        gain_mlp_grad,
        gate_grad,
        up_grad,
        down_grad,
    )


def solution(mesh):
    view = Mesh(mesh.devices.reshape(SIZES), AXES)
    split = P(("xh",) + FSDP)
    rows = P(("xh",) + FSDP, None)
    data = P(FSDP, "xh", None)
    return jax.shard_map(
        on_device,
        mesh=view,
        in_specs=(data, split, rows, rows, rows, rows, split, rows, rows, rows, data),
        out_specs=(data, data, split, rows, rows, rows, rows, split, rows, rows, rows),
        check_vma=False,
    )
```

```python
import functools

import jax
import jax.numpy as jnp
import numpy as np
from jax import lax
from jax.experimental import pallas as pl
from jax.experimental.pallas import tpu as pltpu
from jax.sharding import Mesh, PartitionSpec as P

HEADS = 32
KV_HEADS = 4
HEAD_DIM = 64
EPS = 1e-05
NEG = -1e30
LENGTH = 256
HALF = 128
MIB = 1024 * 1024
M_FLOPS = 1 << 20

AXES = ("xh", "y", "z", "xl", "c")
SIZES = (2, 4, 4, 2, 2)
CHIP_X = ("xh", "xl")
GROUP = ("xl", "xh", "c")
MEMBERS = 8
PAIRED = ("xh", "c")
PLANE = ("y", "z")

bf16 = jnp.bfloat16
f32 = jnp.float32


def contract(a, b, dim_a, dim_b):
    return lax.dot_general(a, b, (((dim_a,), (dim_b,)), ((), ())), preferred_element_type=f32)


def shift(values, axis, by, size):
    return lax.ppermute(values, axis, [(i, (i + by) % size) for i in range(size)])


def together(*values):
    return lax.optimization_barrier(values)


def regroup_to(out_ref, values):
    for k in range(16):
        low = values[:, 64 * k : 64 * k + 64]
        high = values[:, 1024 + 64 * k : 1088 + 64 * k]
        out_ref[:, 128 * k : 128 * (k + 1)] = jnp.concatenate(
            [low[:, :32], high[:, :32], low[:, 32:], high[:, 32:]], axis=1
        )


def regroup_back_to(out_ref, values):
    for k in range(16):
        tile = values[:, 128 * k : 128 * (k + 1)]
        out_ref[:, 64 * k : 64 * k + 64] = jnp.concatenate([tile[:, :32], tile[:, 64:96]], axis=1)
        out_ref[:, 1024 + 64 * k : 1088 + 64 * k] = jnp.concatenate([tile[:, 32:64], tile[:, 96:]], axis=1)


def regroup_kernel(in_ref, out_ref):
    regroup_to(out_ref, in_ref[...])


def regroup(values):
    return call(regroup_kernel, [values.shape], values)[0]


def to_other_core(rows):
    return shift(rows, "c", 1, 2)


def split_sum_kernel(own_ref, got_ref, kept_ref, *sent_refs):
    total = own_ref[...].astype(f32) + got_ref[...].astype(f32)
    rows = kept_ref.shape[0]
    kept_ref[...] = total[:rows]
    for at, sent_ref in enumerate(sent_refs):
        sent_ref[...] = total[rows * (at + 1) : rows * (at + 2)].astype(bf16)


def split_sum(own, got):
    rows, width = HALF, own.shape[1]
    return call(split_sum_kernel, [((rows, width), f32)] + [(rows, width)] * (own.shape[0] // rows - 1), own, got)


def group_gather(rows):
    own = (rows, *together(*(shift(rows, CHIP_X, -ahead, 4) for ahead in (1, 2, 3))))
    return [(block, to_other_core(block)) for block in own]


def line_sum(terms, axis):
    return jnp.sum(lax.all_to_all(terms, axis, 0, 0, tiled=True).astype(f32), axis=0)


def head_rows(flip):
    pairs = []
    for a in range(2):
        for b in range(2):
            for z in range(4):
                for xl in range(2):
                    for c in range(2):
                        source = (((2 * a + b) * 4 + z) * 2 + xl) * 2 + c
                        to_y, to_z = 2 * b + z // 2, 2 * (z % 2) + xl
                        pairs.append((source, ((to_y * 4 + to_z) * 2 + (c ^ flip)) * 2 + a))
    return pairs


def back_rows(flip):
    return [(there, here) for here, there in head_rows(flip)]


FSDP = ("y", "z", "xl", "c")


def rms_scale(values):
    return lax.rsqrt(jnp.mean(values * values, axis=1, keepdims=True) + EPS)


def norm_back(grad_normed, normed, scale_rows, gain):
    scaled = grad_normed * gain
    return scale_rows * (scaled - normed * jnp.mean(scaled * normed, axis=1, keepdims=True))


def resid_kernel(tokens_ref, kept_ref, got_ref, gain_ref, resid_ref, xn_ref):
    resid = tokens_ref[...].astype(f32) + kept_ref[...] + got_ref[...].astype(f32)
    resid_ref[...] = resid
    xn_ref[...] = (resid * rms_scale(resid) * gain_ref[...]).astype(bf16)


def grad_resid_kernel(resid_ref, gain_ref, cot_ref, own_ref, other_ref, *refs):
    grad = own_ref[...].astype(f32) + other_ref[...].astype(f32) + sum(ref[...].astype(f32) for ref in refs[:3])
    resid = resid_ref[...]
    scale = rms_scale(resid)
    grad = cot_ref[...].astype(f32) + norm_back(grad, resid * scale, scale, gain_ref[...])
    refs[3][...] = grad
    refs[4][...] = grad.astype(bf16)


def input_grad_kernel(tokens_ref, gain_ref, grad_resid_ref, kept_ref, got_ref, out_ref):
    inputs = tokens_ref[...].astype(f32)
    scale = rms_scale(inputs)
    grad = kept_ref[...] + got_ref[...].astype(f32)
    regroup_back_to(out_ref, grad_resid_ref[...] + norm_back(grad, inputs * scale, scale, gain_ref[...]))


def block_output_kernel(resid_ref, kept_ref, *refs):
    out = resid_ref[...] + kept_ref[...] + sum(ref[...].astype(f32) for ref in refs[:3])
    regroup_back_to(refs[3], out.astype(bf16))


def out_grad_kernel(kept_ref, given_ref, out_ref):
    regroup_back_to(out_ref, kept_ref[...].astype(f32) + given_ref[...].astype(f32))


def rotate_half(values):
    width = values.shape[1]
    lane = lax.broadcasted_iota(jnp.int32, values.shape, 1) % HEAD_DIM
    later = pltpu.roll(values, width - HEAD_DIM // 2, 1)
    earlier = pltpu.roll(values, HEAD_DIM // 2, 1)
    return jnp.where(lane < HEAD_DIM // 2, -later, earlier)


def head(values, h):
    return values[:, HEAD_DIM * h : HEAD_DIM * (h + 1)]


def allowed_places(first):
    shape = (LENGTH, LENGTH)
    rows = (lax.broadcasted_iota(jnp.int32, shape, 0) + first) & (LENGTH - 1)
    return ((lax.broadcasted_iota(jnp.int32, shape, 1) + first) & (LENGTH - 1)) <= rows


def masked_scores(query, key, allowed):
    return jnp.where(allowed, contract(query, key, 1, 1), NEG)


def wide_table(ref, first, width):
    rows = ref[pl.ds(pl.multiple_of(first, HALF), LENGTH), :]
    return jnp.concatenate([rows] * (width // 128), axis=1)


def out_weights(full_ref):
    for j in range(4):
        width = min(640, 2048 - 640 * j)
        yield full_ref[:, 128 + 32 * j : 160 + 32 * j, :width].reshape(512, width), 640 * j, width


def gain_row(full_ref, which):
    at = 128 * (which + 1)
    return jnp.concatenate([full_ref[y, 224:240, at : at + 128].astype(f32)[:1] for y in range(16)], axis=1)


def gains_kernel(full_ref, *out_refs):
    for which, out_ref in enumerate(out_refs):
        out_ref[...] = gain_row(full_ref, which)


def attend_kernel(first_ref, own_ref, there_ref, full_ref, cos_ref, sin_ref, xn_ref, qkv_ref, level_ref, mixed_ref, out_ref):
    first = first_ref[0]
    cosine, sine = wide_table(cos_ref, first, 512), wide_table(sin_ref, first, 512)
    inputs = jnp.concatenate([own_ref[...], there_ref[...]], axis=0).astype(f32)
    xn_ref[...] = (inputs * rms_scale(inputs) * gain_row(full_ref, 0)).astype(bf16)
    proj = contract(xn_ref[...], full_ref[:, :128, :].reshape(2048, 640), 1, 0).astype(bf16)
    query = proj[:, :512].astype(f32)
    query = (query * cosine + rotate_half(query) * sine).astype(bf16) * bf16(HEAD_DIM**-0.5)
    qkv_ref[:, :512] = query
    wide = proj[:, 512:].astype(f32)
    turned = wide * cosine[:, :128] + rotate_half(wide) * sine[:, :128]
    lane = lax.broadcasted_iota(jnp.int32, wide.shape, 1)
    key_value = jnp.where(lane < HEAD_DIM, turned, wide).astype(bf16)
    qkv_ref[:, 512:] = key_value
    key, value = key_value[:, :HEAD_DIM], key_value[:, HEAD_DIM:]
    allowed = allowed_places(first)
    mixed = []
    for h in range(8):
        scores = masked_scores(head(query, h), key, allowed)
        peak = jnp.max(scores, axis=1, keepdims=True)
        exp_scores = jnp.exp(scores - peak)
        total = jnp.sum(exp_scores, axis=1, keepdims=True)
        mixed.append(contract((exp_scores / total).astype(bf16), value, 1, 0))
        level_ref[:, h : h + 1] = peak + jnp.log(total)
    mixed_ref[...] = jnp.concatenate(mixed, axis=1).astype(bf16)
    for weights, at, width in out_weights(full_ref):
        out_ref[:, at : at + width] = contract(mixed_ref[...], weights, 1, 0).astype(bf16)


def attend_back_kernel(first_ref, own_ref, there_ref, full_ref, cos_ref, sin_ref, qkv_ref, level_ref, out_ref, back_ref):
    first = first_ref[0]
    cosine, sine = wide_table(cos_ref, first, 512), wide_table(sin_ref, first, 512)
    grad = jnp.concatenate([own_ref[...], there_ref[...]], axis=0)
    grad = sum(contract(grad[:, at : at + width], weights, 1, 1) for weights, at, width in out_weights(full_ref))
    grad = grad.astype(bf16)
    query = qkv_ref[:, :512]
    key_value = qkv_ref[:, 512:]
    key, value = key_value[:, :HEAD_DIM], key_value[:, HEAD_DIM:]
    allowed = allowed_places(first)
    grad_key = jnp.zeros((LENGTH, HEAD_DIM), f32)
    grad_value = jnp.zeros((LENGTH, HEAD_DIM), f32)
    grad_query = []
    for h in range(8):
        probs = jnp.exp(masked_scores(head(query, h), key, allowed) - level_ref[:, h : h + 1])
        grad_probs = contract(head(grad, h), value, 1, 1)
        delta = jnp.sum(probs * grad_probs, axis=1, keepdims=True)
        grad_scores = (probs * (grad_probs - delta)).astype(bf16)
        grad_query.append(contract(grad_scores, key, 1, 0))
        grad_key = grad_key + contract(grad_scores, head(query, h), 0, 0)
        grad_value = grad_value + contract(probs.astype(bf16), head(grad, h), 0, 0)
    grad_query = jnp.concatenate(grad_query, axis=1) * HEAD_DIM**-0.5
    out_ref[:, :512] = (grad_query * cosine - rotate_half(grad_query * sine)).astype(bf16)
    wide = jnp.concatenate([grad_key, grad_value], axis=1)
    turned = wide * cosine[:, :128] - rotate_half(wide * sine[:, :128])
    lane = lax.broadcasted_iota(jnp.int32, wide.shape, 1)
    out_ref[:, 512:] = jnp.where(lane < HEAD_DIM, turned, wide).astype(bf16)
    back_ref[...] = contract(out_ref[...], full_ref[:, :128, :].reshape(2048, 640), 1, 1).astype(bf16)


def call(kernel, outs, *arrays, grid=(), in_specs=None, out_specs=None, hbm=False, held=(), flops=1 << 20, scratch=(), vmem_mib=20):
    kind = pltpu.HBM if hbm else jax.ShapeDtypeStruct
    outs = [out if isinstance(out[1], type) or hasattr(out[1], "dtype") else (out, bf16) for out in outs]
    vmem, smem, block = pl.BlockSpec(memory_space=pltpu.VMEM), pl.BlockSpec(memory_space=pltpu.SMEM), pl.BlockSpec()
    if in_specs is None:
        in_specs = [smem if a.dtype == jnp.int32 else vmem if at in held else block for at, a in enumerate(arrays)]
    return pl.pallas_call(
        kernel,
        out_shape=[kind(shape, dtype) for shape, dtype in outs],
        grid=grid,
        in_specs=in_specs,
        out_specs=out_specs or [block] * len(outs),
        scratch_shapes=scratch,
        compiler_params=pltpu.CompilerParams(vmem_limit_bytes=vmem_mib * MIB),
        cost_estimate=pl.CostEstimate(flops=flops, bytes_accessed=1024, transcendentals=0),
    )(*arrays)


def mlp_kernel(part, own_ref, other_ref, own_cot_ref, other_cot_ref, w_ref, hidden_ref, grad_ref, back_ref, back_other_ref):
    xn = jnp.concatenate([own_ref[...], other_ref[...]], axis=0)
    cot = jnp.concatenate([own_cot_ref[...], other_cot_ref[...]], axis=0)
    wide = contract(xn, w_ref[:, : 2 * part], 1, 0)
    grad_hidden = contract(cot, w_ref[:, 2 * part :], 1, 0)
    gate, up = wide[:, :part], wide[:, part:]
    sigmoid_gate = jax.nn.sigmoid(gate)
    silu_gate = gate * sigmoid_gate
    hidden_ref[...] = (silu_gate * up).astype(bf16)
    grad_ref[:, :part] = (
        grad_hidden * up * (sigmoid_gate * (1.0 + gate * (1.0 - sigmoid_gate)))
    ).astype(bf16)
    grad_ref[:, part:] = (grad_hidden * silu_gate).astype(bf16)
    back = contract(grad_ref[...], w_ref[:, : 2 * part], 1, 1).astype(bf16)
    rows = own_ref.shape[0]
    back_ref[...] = back[:rows]
    back_other_ref[...] = back[rows:]


def mlp_out_kernel(part, *refs):
    hidden_refs, w_ref, out_refs = refs[:4], refs[4], refs[5:]
    for chip in range(4):
        out = contract(hidden_refs[chip][...], w_ref[:, 2 * part :], 1, 1).astype(bf16)
        rows = out.shape[0] // 2
        for core in range(2):
            out_refs[core][rows * chip : rows * (chip + 1), :] = out[rows * core : rows * (core + 1)]


def mlp_terms_kernel(part, *refs):
    xn, cot, grad, hidden = [
        jnp.concatenate([ref[...] for ref in group], axis=0) for group in (refs[:8], refs[8:16], refs[16:20], refs[20:24])
    ]
    out_ref = refs[24]
    out_ref[:, : 2 * part] = contract(xn, grad, 0, 0).astype(bf16)
    out_ref[:, 2 * part :] = contract(cot, hidden, 0, 0).astype(bf16)


def columns_spec(rows, block):
    return pl.BlockSpec((rows, block), lambda i: (0, i))


def whole_spec(array):
    return pl.BlockSpec(array.shape, lambda i: (0, 0), pipeline_mode=pl.Buffered(1))


def mlp_terms(part, xn, cot, grad, hidden):
    rows, width = xn[0].shape
    block = 512
    return call(
        functools.partial(mlp_terms_kernel, part),
        [(width, 3 * part)],
        *xn,
        *cot,
        *grad,
        *hidden,
        grid=(width // block,),
        in_specs=[columns_spec(rows, block)] * 16 + [whole_spec(a) for a in grad + hidden],
        out_specs=[pl.BlockSpec((block, 3 * part), lambda i: (i, 0))],
        hbm=True,
        vmem_mib=32,
    )[0]


def out_terms_kernel(place_ref, mixed_ref, mixed_other_ref, *refs):
    own, other = [jnp.concatenate([ref[...] for ref in pair], axis=0) for pair in (refs[:2], refs[2:4])]
    terms_ref, out_refs = refs[8], refs[4:8]
    terms_ref[...] = (contract(mixed_ref[...], own, 0, 0) + contract(mixed_other_ref[...], other, 0, 0)).astype(bf16)
    for ahead, out_ref in enumerate(out_refs):
        at = (place_ref[0] + ahead) % 4
        for y in range(4):
            out_ref[y] = terms_ref[pl.ds(pl.multiple_of((4 * y + at) * 32, 32), 32), :]


def out_terms(place, mixed, grad):
    rows, width = grad[0][0].shape
    block = 512
    blocks = [columns_spec(rows, block)] * 4
    return call(
        out_terms_kernel,
        [(4, 32, width)] * 4,
        place.astype(jnp.int32)[None],
        *mixed,
        *grad[0],
        *grad[1],
        grid=(width // block,),
        in_specs=[pl.BlockSpec(memory_space=pltpu.SMEM)] + [whole_spec(a) for a in mixed] + blocks,
        out_specs=[pl.BlockSpec((4, 32, block), lambda i: (0, 0, i))] * 4,
        scratch=[pltpu.VMEM((512, block), bf16)],
    )


def qkv_terms_kernel(xn_ref, xn_other_ref, grad_ref, grad_other_ref, out_ref):
    out_ref[...] = (
        contract(xn_ref[...], grad_ref[...], 0, 0) + contract(xn_other_ref[...], grad_other_ref[...], 0, 0)
    ).astype(bf16)


def qkv_terms(xn, grad):
    rows, width = xn[0].shape
    block = 1024
    return call(
        qkv_terms_kernel,
        [(width, 640)],
        *xn,
        *grad,
        grid=(width // block,),
        in_specs=[columns_spec(rows, block)] * 2 + [whole_spec(a) for a in grad],
        out_specs=[pl.BlockSpec((block, 640), lambda i: (i, 0))],
        hbm=True,
    )[0]


def line_terms_kernel(place_ref, in_ref, *out_refs):
    for ahead, out_ref in enumerate(out_refs):
        at = (place_ref[0] + ahead) % 4
        out_ref[...] = sum(in_ref[y, at].astype(f32) for y in range(4)).astype(bf16)


def line_terms(gathered, place):
    return call(line_terms_kernel, [gathered.shape[2:]] * 4, place.astype(jnp.int32)[None], gathered, flops=64 << 30)


def shifted(terms, axis):
    return [terms[0]] + [shift(terms[ahead], axis, ahead, 4) for ahead in (1, 2, 3)]


def sum_kernel(*refs):
    refs[-1][...] = sum(ref[...].astype(f32) for ref in refs[:-1]).astype(bf16)


def shares_kernel(mlp_ref, *refs):
    out_ref = refs[-1]
    total = sum(ref[...].astype(f32) for ref in refs[:-1]).astype(bf16)
    rows = out_ref.shape[1]
    for member in range(MEMBERS):
        out_ref[member, :, :640] = total[rows * member : rows * (member + 1)]
        out_ref[member, :, 640:] = mlp_ref[rows * member : rows * (member + 1), :]


def ring_terms_kernel(place_ref, *refs):
    for ahead, out_ref in enumerate(refs[4:]):
        at = (place_ref[0] + ahead) % 4
        out_ref[...] = sum(ref[at].astype(f32) for ref in refs[:4]).astype(bf16)


def unpack_kernel(part, in_ref, gate_ref, up_ref, down_ref, query_ref, key_ref, value_ref):
    for member in range(MEMBERS):
        for place, out_ref in enumerate((gate_ref, up_ref, down_ref)):
            at = 640 + part * place
            out_ref[:, part * member : part * (member + 1)] = in_ref[member, :, at : at + part].astype(f32)
    for own in range(4):
        total = in_ref[own, :, :640].astype(f32) + in_ref[own + 4, :, :640].astype(f32)
        query_ref[:, 512 * own : 512 * (own + 1)] = total[:, :512]
        key_ref[:, HEAD_DIM * own : HEAD_DIM * (own + 1)] = total[:, 512 : 512 + HEAD_DIM]
        value_ref[:, HEAD_DIM * own : HEAD_DIM * (own + 1)] = total[:, 512 + HEAD_DIM :]


def attn_pack_kernel(query_ref, key_ref, value_ref, gains_ref, out_ref):
    for member in range(MEMBERS):
        own = member % 4
        out_ref[member, :, :512] = query_ref[:, 512 * own : 512 * (own + 1)]
        out_ref[member, :, 512:640] = jnp.concatenate([head(key_ref, own), head(value_ref, own)], axis=1)
        out_ref[member, :, 640:768] = gains_ref[...]


def mlp_pack_kernel(part, gate_ref, up_ref, down_ref, out_ref):
    for member in range(MEMBERS):
        for place, ref in enumerate((gate_ref, up_ref, down_ref)):
            out_ref[member, :, part * place : part * (place + 1)] = ref[:, part * member : part * (member + 1)]


def rotary_tables():
    half = HEAD_DIM // 2
    frequency = 10000.0 ** (-2.0 * np.arange(half) / HEAD_DIM)
    places = np.arange(LENGTH + HALF) % LENGTH
    angles = np.tile(places[:, None] * frequency[None, :], (1, 4))
    return np.cos(angles).astype(np.float32), np.sin(angles).astype(np.float32)


def on_device(
    tokens, gain_attn, w_query, w_key, w_value, w_out, gain_mlp, w_gate, w_up, w_down, cotangent
):
    own_rows = w_query.shape[0]
    part = w_gate.shape[1] // MEMBERS

    gains = jnp.pad(jnp.concatenate([gain_attn, gain_mlp])[None, :], ((0, own_rows - 1), (0, 128 - 2 * own_rows)))
    block = call(attn_pack_kernel, [(MEMBERS, own_rows, 768)], w_query, w_key, w_value, gains)[0]
    out_block = regroup(w_out)
    block, here, there = together(
        lax.all_to_all(block, GROUP, 0, 0, tiled=True),
        lax.ppermute(out_block, FSDP, head_rows(0)),
        lax.ppermute(out_block, FSDP, head_rows(1)),
    )
    left = lax.axis_index("xl") == 0
    out_block = jnp.concatenate([jnp.where(left, here, there), jnp.where(left, there, here)], axis=0)
    gains = block[:, 0, 640 : 640 + 2 * own_rows].reshape(MEMBERS, 2, own_rows).swapaxes(0, 1).reshape(1, 256)
    gains = jnp.pad(gains, ((0, 2 * own_rows - 1), (0, 256)))
    attn_block = jnp.concatenate(
        [block[:, :, :640].reshape(MEMBERS * own_rows, 640)]
        + [out_block[:, 640 * j : 640 * (j + 1)] for j in range(3)]
        + [jnp.concatenate([out_block[:, 1920:], gains], axis=1)],
        axis=0,
    )
    mlp_block = call(functools.partial(mlp_pack_kernel, part), [(MEMBERS, own_rows, 3 * part)], w_gate, w_up, w_down)[0]
    mlp_block, attn_block = together(mlp_block, attn_block)
    attn_full = lax.all_gather(attn_block, PLANE, axis=0)
    own_tokens, own_cotangent = regroup(tokens[0]), regroup(cotangent[0])
    mlp_block, there_tokens, own_cotangent = together(
        lax.all_to_all(mlp_block, GROUP, 0, 0, tiled=True), shift(own_tokens, "xh", 1, 2), own_cotangent
    )
    mlp_block = mlp_block.reshape(MEMBERS * own_rows, 3 * part)
    mlp_w = lax.all_gather(mlp_block, PLANE, axis=0, tiled=True)

    pair_tokens = (own_tokens, there_tokens), (to_other_core(own_tokens), to_other_core(there_tokens))
    attn_full, pair_tokens, group_cotangent = together(attn_full, pair_tokens, group_gather(own_cotangent))
    gain_one, gain_two = call(gains_kernel, [((1, 2048), f32)] * 2, attn_full, held=(0,))

    first = (HALF * lax.axis_index("xh")).astype(jnp.int32)[None]
    cosine, sine = rotary_tables()

    def attend(chunks):
        shapes = [(LENGTH, 2048), (LENGTH, 640), ((LENGTH, 8), f32), (LENGTH, 512), (LENGTH, 2048)]
        return call(attend_kernel, shapes, first, *chunks, attn_full, cosine, sine, held=(3,))

    xn_other, qkv_other, level_other, mixed_other, out_other = attend(pair_tokens[1])
    xn_own, qkv_own, level_own, mixed_own, out_own = attend(pair_tokens[0])
    kept, sent = split_sum(out_own, to_other_core(out_other))
    resid, xn_rows = call(
        resid_kernel, [((HALF, 2048), f32), (HALF, 2048)], own_tokens, kept, shift(sent, "xh", 1, 2), gain_two
    )

    def feed_forward(chip):
        shapes = [(LENGTH, part), (LENGTH, 2 * part), (HALF, 2048), (HALF, 2048)]
        return call(functools.partial(mlp_kernel, part), shapes, *xn_two[chip], *group_cotangent[chip], mlp_w, held=(4,), flops=M_FLOPS)

    arrived = together(*(shift(xn_rows, CHIP_X, -ahead, 4) for ahead in (1, 2, 3)))
    xn_two = [(rows, to_other_core(rows)) for rows in (xn_rows, *arrived)]
    results, got = [None] * 4, [None] * 4

    def core_total(ahead):
        return (results[ahead][2].astype(f32) + to_other_core(results[ahead][3]).astype(f32)).astype(bf16)

    results[2] = feed_forward(2)
    results[3] = feed_forward(3)
    far, xn_one_ahead = together(core_total(2), xn_two[1][0])
    xn_two[1] = xn_one_ahead, xn_two[1][1]
    results[1] = feed_forward(1)
    near, xn_own_rows = together(core_total(3), xn_rows)
    xn_two[0] = xn_own_rows, xn_two[0][1]
    got[3] = shift(near, CHIP_X, 3, 4)
    results[0], got[2] = together(feed_forward(0), shift(far, CHIP_X, 2, 4))
    got[1] = shift(core_total(1), CHIP_X, 1, 4)
    hidden, grad_wide, backs, back_others = (list(kind) for kind in zip(*results))
    flat = [[block for pair in pairs for block in pair] for pairs in (xn_two, group_cotangent)]
    own_other, got[1], got[3], mlp_term = together(
        to_other_core(back_others[0]), got[1], got[3], mlp_terms(part, *flat, grad_wide, hidden)
    )
    shares = lax.psum_scatter(mlp_term, PLANE, scatter_dimension=0, tiled=True)
    grad_resid, grad_rows = call(
        grad_resid_kernel,
        [((HALF, 2048), f32), (HALF, 2048)],
        *(resid, gain_two, own_cotangent, backs[0], own_other, *got[1:]),
    )
    grad_rows, hidden[0] = together(grad_rows, hidden[0])
    out_own, out_other = call(functools.partial(mlp_out_kernel, part), [(4 * HALF, 2048)] * 2, *hidden, mlp_w)
    grad_there, grad_rows_other, out_own, out_other = together(
        shift(grad_rows, "xh", 1, 2), to_other_core(grad_rows), out_own, out_other
    )
    grad_attn = (grad_rows, grad_there), (grad_rows_other, to_other_core(grad_there))

    def attend_back(chunks, qkv, level):
        shapes = [(LENGTH, 640), (LENGTH, 2048)]
        return call(attend_back_kernel, shapes, first, *chunks, attn_full, cosine, sine, qkv, level, held=(3,))

    (grad_own, back_own), other_chunks, (out_kept, *out_sent) = together(
        attend_back(grad_attn[0], qkv_own, level_own), grad_attn[1], split_sum(out_own, to_other_core(out_other))
    )
    grad_other, back_other = attend_back(other_chunks, qkv_other, level_other)
    attn_term = qkv_terms((xn_own, xn_other), (grad_own, grad_other)).reshape(4, 4, 8 * own_rows, 640)
    attn_term, back_own, grad_attn = together(attn_term, back_own, grad_attn)
    kept, sent = split_sum(back_own, to_other_core(back_other))
    out_term = out_terms(lax.axis_index("z"), (mixed_own, mixed_other), grad_attn)
    out_got = [shift(rows, CHIP_X, ahead, 4) for ahead, rows in zip((1, 2, 3), out_sent)]
    grad_got = shift(sent, "xh", 1, 2)
    place_y = lax.axis_index("y").astype(jnp.int32)[None]
    attn_terms, out_term, out_got = together(
        line_terms(lax.all_to_all(attn_term, "y", 0, 0, tiled=True), lax.axis_index("z")),
        shifted(out_term, "z"),
        out_got,
    )
    shares = call(
        shares_kernel, [(MEMBERS, own_rows, 640 + 3 * part)], shares, *shifted(attn_terms, "z")
    )[0]
    block_output = call(block_output_kernel, [(HALF, 2048)], resid, out_kept, *out_got)[0]
    shares, out_term, grad_got, block_output = together(shares, out_term, grad_got, block_output)
    out_term = call(ring_terms_kernel, [(2 * own_rows, 2048)] * 4, place_y, *out_term)
    out_share = call(sum_kernel, [(2 * own_rows, 2048)], *shifted(out_term, "y"))[0]
    input_grad = call(input_grad_kernel, [((HALF, 2048), f32)], own_tokens, gain_one, grad_resid, kept, grad_got)[0]
    taken = jnp.where(left, out_share[:own_rows], out_share[own_rows:])
    given = jnp.where(left, out_share[own_rows:], out_share[:own_rows])
    taken = lax.ppermute(taken, FSDP, back_rows(0))
    given = lax.ppermute(given, FSDP, back_rows(1))
    shares, block_output, input_grad = together(
        call(
            functools.partial(unpack_kernel, part),
            [((own_rows, MEMBERS * part), f32)] * 3
            + [((own_rows, 2048), f32), ((own_rows, 256), f32), ((own_rows, 256), f32)],
            lax.all_to_all(shares, GROUP, 0, 0, tiled=True),
            flops=64 << 30,
        ),
        block_output,
        input_grad,
    )
    gate_grad, up_grad, down_grad, query_grad, key_grad, value_grad = shares
    def gain_grad(gain, *pairs):
        total = sum(jnp.sum(w.astype(f32) * grad, axis=1) for w, grad in pairs)
        return total / gain.astype(f32)

    gain_attn_grad = gain_grad(gain_attn, (w_query, query_grad), (w_key, key_grad), (w_value, value_grad))
    gain_mlp_grad = gain_grad(gain_mlp, (w_gate, gate_grad), (w_up, up_grad))
    gain_attn_grad, gain_mlp_grad, taken, given = together(gain_attn_grad, gain_mlp_grad, taken, given)
    out_grad = call(out_grad_kernel, [((own_rows, 2048), f32)], taken, given)[0]
    return (
        block_output[None],
        input_grad[None],
        gain_attn_grad,
        query_grad,
        key_grad,
        value_grad,
        out_grad,
        gain_mlp_grad,
        gate_grad,
        up_grad,
        down_grad,
    )


def solution(mesh):
    view = Mesh(mesh.devices.reshape(SIZES), AXES)
    split = P(("xh",) + FSDP)
    rows = P(("xh",) + FSDP, None)
    data = P(FSDP, "xh", None)
    return jax.shard_map(
        on_device,
        mesh=view,
        in_specs=(data, split, rows, rows, rows, rows, split, rows, rows, rows, data),
        out_specs=(data, data, split, rows, rows, rows, rows, split, rows, rows, rows),
        check_vma=False,
    )
```

```python
import functools

import jax
import jax.numpy as jnp
import numpy as np
from jax import lax
from jax.experimental import pallas as pl
from jax.experimental.pallas import tpu as pltpu
from jax.sharding import Mesh, PartitionSpec as P

HEADS = 32
KV_HEADS = 4
HEAD_DIM = 64
EPS = 1e-05
NEG = -1e30
LENGTH = 256
HALF = 128
MIB = 1024 * 1024
M_FLOPS = 1 << 20

AXES = ("xh", "y", "z", "xl", "c")
SIZES = (2, 4, 4, 2, 2)
CHIP_X = ("xh", "xl")
GROUP = ("xl", "xh", "c")
MEMBERS = 8
PAIRED = ("xh", "c")
PLANE = ("y", "z")

bf16 = jnp.bfloat16
f32 = jnp.float32


def contract(a, b, dim_a, dim_b):
    return lax.dot_general(a, b, (((dim_a,), (dim_b,)), ((), ())), preferred_element_type=f32)


def shift(values, axis, by, size):
    return lax.ppermute(values, axis, [(i, (i + by) % size) for i in range(size)])


def together(*values):
    return lax.optimization_barrier(values)


def regroup_to(out_ref, values):
    for k in range(16):
        low = values[:, 64 * k : 64 * k + 64]
        high = values[:, 1024 + 64 * k : 1088 + 64 * k]
        out_ref[:, 128 * k : 128 * (k + 1)] = jnp.concatenate(
            [low[:, :32], high[:, :32], low[:, 32:], high[:, 32:]], axis=1
        )


def regroup_back_to(out_ref, values):
    for k in range(16):
        tile = values[:, 128 * k : 128 * (k + 1)]
        out_ref[:, 64 * k : 64 * k + 64] = jnp.concatenate([tile[:, :32], tile[:, 64:96]], axis=1)
        out_ref[:, 1024 + 64 * k : 1088 + 64 * k] = jnp.concatenate([tile[:, 32:64], tile[:, 96:]], axis=1)


def regroup_kernel(in_ref, out_ref):
    regroup_to(out_ref, in_ref[...])


def regroup(values):
    return call(regroup_kernel, [values.shape], values)[0]


def to_other_core(rows):
    return shift(rows, "c", 1, 2)


def split_sum_kernel(own_ref, got_ref, kept_ref, *sent_refs):
    total = own_ref[...].astype(f32) + got_ref[...].astype(f32)
    rows = kept_ref.shape[0]
    kept_ref[...] = total[:rows]
    for at, sent_ref in enumerate(sent_refs):
        sent_ref[...] = total[rows * (at + 1) : rows * (at + 2)].astype(bf16)


def split_sum(own, got):
    rows, width = HALF, own.shape[1]
    return call(split_sum_kernel, [((rows, width), f32)] + [(rows, width)] * (own.shape[0] // rows - 1), own, got)


def group_gather(rows):
    own = (rows, *together(*(shift(rows, CHIP_X, -ahead, 4) for ahead in (1, 2, 3))))
    return [(block, to_other_core(block)) for block in own]


def line_sum(terms, axis):
    return jnp.sum(lax.all_to_all(terms, axis, 0, 0, tiled=True).astype(f32), axis=0)


def head_rows(flip):
    pairs = []
    for a in range(2):
        for b in range(2):
            for z in range(4):
                for xl in range(2):
                    for c in range(2):
                        source = (((2 * a + b) * 4 + z) * 2 + xl) * 2 + c
                        to_y, to_z = 2 * b + z // 2, 2 * (z % 2) + xl
                        pairs.append((source, ((to_y * 4 + to_z) * 2 + (c ^ flip)) * 2 + a))
    return pairs


def back_rows(flip):
    return [(there, here) for here, there in head_rows(flip)]


FSDP = ("y", "z", "xl", "c")


def rms_scale(values):
    return lax.rsqrt(jnp.mean(values * values, axis=1, keepdims=True) + EPS)


def norm_back(grad_normed, normed, scale_rows, gain):
    scaled = grad_normed * gain
    return scale_rows * (scaled - normed * jnp.mean(scaled * normed, axis=1, keepdims=True))


def resid_kernel(tokens_ref, kept_ref, got_ref, gain_ref, resid_ref, xn_ref):
    resid = tokens_ref[...].astype(f32) + kept_ref[...] + got_ref[...].astype(f32)
    resid_ref[...] = resid
    xn_ref[...] = (resid * rms_scale(resid) * gain_ref[...]).astype(bf16)


def grad_resid_kernel(resid_ref, gain_ref, cot_ref, own_ref, other_ref, *refs):
    grad = own_ref[...].astype(f32) + other_ref[...].astype(f32) + sum(ref[...].astype(f32) for ref in refs[:3])
    resid = resid_ref[...]
    scale = rms_scale(resid)
    grad = cot_ref[...].astype(f32) + norm_back(grad, resid * scale, scale, gain_ref[...])
    refs[3][...] = grad
    refs[4][...] = grad.astype(bf16)


def input_grad_kernel(tokens_ref, gain_ref, grad_resid_ref, kept_ref, got_ref, out_ref):
    inputs = tokens_ref[...].astype(f32)
    scale = rms_scale(inputs)
    grad = kept_ref[...] + got_ref[...].astype(f32)
    regroup_back_to(out_ref, grad_resid_ref[...] + norm_back(grad, inputs * scale, scale, gain_ref[...]))


def block_output_kernel(resid_ref, kept_ref, *refs):
    out = resid_ref[...] + kept_ref[...] + sum(ref[...].astype(f32) for ref in refs[:3])
    regroup_back_to(refs[3], out.astype(bf16))


def out_grad_kernel(kept_ref, given_ref, out_ref):
    regroup_back_to(out_ref, kept_ref[...].astype(f32) + given_ref[...].astype(f32))


def rotate_half(values):
    width = values.shape[1]
    lane = lax.broadcasted_iota(jnp.int32, values.shape, 1) % HEAD_DIM
    later = pltpu.roll(values, width - HEAD_DIM // 2, 1)
    earlier = pltpu.roll(values, HEAD_DIM // 2, 1)
    return jnp.where(lane < HEAD_DIM // 2, -later, earlier)


def head(values, h):
    return values[:, HEAD_DIM * h : HEAD_DIM * (h + 1)]


def allowed_places(first):
    shape = (LENGTH, LENGTH)
    rows = (lax.broadcasted_iota(jnp.int32, shape, 0) + first) & (LENGTH - 1)
    return ((lax.broadcasted_iota(jnp.int32, shape, 1) + first) & (LENGTH - 1)) <= rows


def probabilities(query, key, allowed):
    scores = jnp.where(allowed, contract(query, key, 1, 1) * HEAD_DIM**-0.5, NEG)
    exp_scores = jnp.exp(scores - jnp.max(scores, axis=1, keepdims=True))
    return exp_scores / jnp.sum(exp_scores, axis=1, keepdims=True)


def wide_table(ref, first, width):
    rows = ref[pl.ds(pl.multiple_of(first, HALF), LENGTH), :]
    return jnp.concatenate([rows] * (width // 128), axis=1)


def out_weights(full_ref):
    for j in range(4):
        width = min(640, 2048 - 640 * j)
        yield full_ref[:, 128 + 32 * j : 160 + 32 * j, :width].reshape(512, width), 640 * j, width


def gain_row(full_ref, which):
    at = 128 * (which + 1)
    return jnp.concatenate([full_ref[y, 224:240, at : at + 128].astype(f32)[:1] for y in range(16)], axis=1)


def gains_kernel(full_ref, *out_refs):
    for which, out_ref in enumerate(out_refs):
        out_ref[...] = gain_row(full_ref, which)


def attend_kernel(first_ref, own_ref, there_ref, full_ref, cos_ref, sin_ref, xn_ref, qkv_ref, mixed_ref, out_ref):
    first = first_ref[0]
    cosine, sine = wide_table(cos_ref, first, 512), wide_table(sin_ref, first, 512)
    inputs = jnp.concatenate([own_ref[...], there_ref[...]], axis=0).astype(f32)
    xn_ref[...] = (inputs * rms_scale(inputs) * gain_row(full_ref, 0)).astype(bf16)
    proj = contract(xn_ref[...], full_ref[:, :128, :].reshape(2048, 640), 1, 0).astype(bf16)
    query = proj[:, :512].astype(f32)
    query = (query * cosine + rotate_half(query) * sine).astype(bf16)
    qkv_ref[:, :512] = query
    wide = proj[:, 512:].astype(f32)
    turned = wide * cosine[:, :128] + rotate_half(wide) * sine[:, :128]
    lane = lax.broadcasted_iota(jnp.int32, wide.shape, 1)
    key_value = jnp.where(lane < HEAD_DIM, turned, wide).astype(bf16)
    qkv_ref[:, 512:] = key_value
    key, value = key_value[:, :HEAD_DIM], key_value[:, HEAD_DIM:]
    allowed = allowed_places(first)
    mixed = [
        contract(probabilities(head(query, h), key, allowed).astype(bf16), value, 1, 0) for h in range(8)
    ]
    mixed_ref[...] = jnp.concatenate(mixed, axis=1).astype(bf16)
    for weights, at, width in out_weights(full_ref):
        out_ref[:, at : at + width] = contract(mixed_ref[...], weights, 1, 0).astype(bf16)


def attend_back_kernel(first_ref, own_ref, there_ref, full_ref, cos_ref, sin_ref, qkv_ref, out_ref, back_ref):
    first = first_ref[0]
    cosine, sine = wide_table(cos_ref, first, 512), wide_table(sin_ref, first, 512)
    grad = jnp.concatenate([own_ref[...], there_ref[...]], axis=0)
    grad = sum(contract(grad[:, at : at + width], weights, 1, 1) for weights, at, width in out_weights(full_ref))
    grad = grad.astype(bf16)
    query = qkv_ref[:, :512]
    key_value = qkv_ref[:, 512:]
    key, value = key_value[:, :HEAD_DIM], key_value[:, HEAD_DIM:]
    allowed = allowed_places(first)
    grad_key = jnp.zeros((LENGTH, HEAD_DIM), f32)
    grad_value = jnp.zeros((LENGTH, HEAD_DIM), f32)
    grad_query = []
    for h in range(8):
        probs = probabilities(head(query, h), key, allowed)
        grad_probs = contract(head(grad, h), value, 1, 1)
        delta = jnp.sum(probs * grad_probs, axis=1, keepdims=True)
        grad_scores = (probs * (grad_probs - delta)).astype(bf16)
        grad_query.append(contract(grad_scores, key, 1, 0))
        grad_key = grad_key + contract(grad_scores, head(query, h), 0, 0)
        grad_value = grad_value + contract(probs.astype(bf16), head(grad, h), 0, 0)
    grad_query = jnp.concatenate(grad_query, axis=1) * HEAD_DIM**-0.5
    out_ref[:, :512] = (grad_query * cosine - rotate_half(grad_query * sine)).astype(bf16)
    wide = jnp.concatenate([grad_key * HEAD_DIM**-0.5, grad_value], axis=1)
    turned = wide * cosine[:, :128] - rotate_half(wide * sine[:, :128])
    lane = lax.broadcasted_iota(jnp.int32, wide.shape, 1)
    out_ref[:, 512:] = jnp.where(lane < HEAD_DIM, turned, wide).astype(bf16)
    back_ref[...] = contract(out_ref[...], full_ref[:, :128, :].reshape(2048, 640), 1, 1).astype(bf16)


def call(kernel, outs, *arrays, grid=(), in_specs=None, out_specs=None, hbm=False, held=(), flops=1 << 20, scratch=(), vmem_mib=20):
    kind = pltpu.HBM if hbm else jax.ShapeDtypeStruct
    outs = [out if isinstance(out[1], type) or hasattr(out[1], "dtype") else (out, bf16) for out in outs]
    vmem, smem, block = pl.BlockSpec(memory_space=pltpu.VMEM), pl.BlockSpec(memory_space=pltpu.SMEM), pl.BlockSpec()
    if in_specs is None:
        in_specs = [smem if a.dtype == jnp.int32 else vmem if at in held else block for at, a in enumerate(arrays)]
    return pl.pallas_call(
        kernel,
        out_shape=[kind(shape, dtype) for shape, dtype in outs],
        grid=grid,
        in_specs=in_specs,
        out_specs=out_specs or [block] * len(outs),
        scratch_shapes=scratch,
        compiler_params=pltpu.CompilerParams(vmem_limit_bytes=vmem_mib * MIB),
        cost_estimate=pl.CostEstimate(flops=flops, bytes_accessed=1024, transcendentals=0),
    )(*arrays)


def mlp_kernel(part, own_ref, other_ref, own_cot_ref, other_cot_ref, w_ref, hidden_ref, grad_ref, back_ref, back_other_ref):
    xn = jnp.concatenate([own_ref[...], other_ref[...]], axis=0)
    cot = jnp.concatenate([own_cot_ref[...], other_cot_ref[...]], axis=0)
    wide = contract(xn, w_ref[:, : 2 * part], 1, 0)
    grad_hidden = contract(cot, w_ref[:, 2 * part :], 1, 0)
    gate, up = wide[:, :part], wide[:, part:]
    sigmoid_gate = jax.nn.sigmoid(gate)
    silu_gate = gate * sigmoid_gate
    hidden_ref[...] = (silu_gate * up).astype(bf16)
    grad_ref[:, :part] = (
        grad_hidden * up * (sigmoid_gate * (1.0 + gate * (1.0 - sigmoid_gate)))
    ).astype(bf16)
    grad_ref[:, part:] = (grad_hidden * silu_gate).astype(bf16)
    back = contract(grad_ref[...], w_ref[:, : 2 * part], 1, 1).astype(bf16)
    rows = own_ref.shape[0]
    back_ref[...] = back[:rows]
    back_other_ref[...] = back[rows:]


def mlp_out_kernel(part, *refs):
    hidden_refs, w_ref, out_refs = refs[:4], refs[4], refs[5:]
    for chip in range(4):
        out = contract(hidden_refs[chip][...], w_ref[:, 2 * part :], 1, 1).astype(bf16)
        rows = out.shape[0] // 2
        for core in range(2):
            out_refs[core][rows * chip : rows * (chip + 1), :] = out[rows * core : rows * (core + 1)]


def mlp_terms_kernel(part, *refs):
    xn, cot, grad, hidden = [
        jnp.concatenate([ref[...] for ref in group], axis=0) for group in (refs[:8], refs[8:16], refs[16:20], refs[20:24])
    ]
    out_ref = refs[24]
    out_ref[:, : 2 * part] = contract(xn, grad, 0, 0).astype(bf16)
    out_ref[:, 2 * part :] = contract(cot, hidden, 0, 0).astype(bf16)


def columns_spec(rows, block):
    return pl.BlockSpec((rows, block), lambda i: (0, i))


def whole_spec(array):
    return pl.BlockSpec(array.shape, lambda i: (0, 0), pipeline_mode=pl.Buffered(1))


def mlp_terms(part, xn, cot, grad, hidden):
    rows, width = xn[0].shape
    block = 512
    return call(
        functools.partial(mlp_terms_kernel, part),
        [(width, 3 * part)],
        *xn,
        *cot,
        *grad,
        *hidden,
        grid=(width // block,),
        in_specs=[columns_spec(rows, block)] * 16 + [whole_spec(a) for a in grad + hidden],
        out_specs=[pl.BlockSpec((block, 3 * part), lambda i: (i, 0))],
        hbm=True,
        vmem_mib=32,
    )[0]


def out_terms_kernel(place_ref, mixed_ref, mixed_other_ref, *refs):
    own, other = [jnp.concatenate([ref[...] for ref in pair], axis=0) for pair in (refs[:2], refs[2:4])]
    terms_ref, out_refs = refs[8], refs[4:8]
    terms_ref[...] = (contract(mixed_ref[...], own, 0, 0) + contract(mixed_other_ref[...], other, 0, 0)).astype(bf16)
    for ahead, out_ref in enumerate(out_refs):
        at = (place_ref[0] + ahead) % 4
        for y in range(4):
            out_ref[y] = terms_ref[pl.ds(pl.multiple_of((4 * y + at) * 32, 32), 32), :]


def out_terms(place, mixed, grad):
    rows, width = grad[0][0].shape
    block = 512
    blocks = [columns_spec(rows, block)] * 4
    return call(
        out_terms_kernel,
        [(4, 32, width)] * 4,
        place.astype(jnp.int32)[None],
        *mixed,
        *grad[0],
        *grad[1],
        grid=(width // block,),
        in_specs=[pl.BlockSpec(memory_space=pltpu.SMEM)] + [whole_spec(a) for a in mixed] + blocks,
        out_specs=[pl.BlockSpec((4, 32, block), lambda i: (0, 0, i))] * 4,
        scratch=[pltpu.VMEM((512, block), bf16)],
    )


def qkv_terms_kernel(xn_ref, xn_other_ref, grad_ref, grad_other_ref, out_ref):
    out_ref[...] = (
        contract(xn_ref[...], grad_ref[...], 0, 0) + contract(xn_other_ref[...], grad_other_ref[...], 0, 0)
    ).astype(bf16)


def qkv_terms(xn, grad):
    rows, width = xn[0].shape
    block = 1024
    return call(
        qkv_terms_kernel,
        [(width, 640)],
        *xn,
        *grad,
        grid=(width // block,),
        in_specs=[columns_spec(rows, block)] * 2 + [whole_spec(a) for a in grad],
        out_specs=[pl.BlockSpec((block, 640), lambda i: (i, 0))],
        hbm=True,
    )[0]


def line_terms_kernel(place_ref, in_ref, *out_refs):
    for ahead, out_ref in enumerate(out_refs):
        at = (place_ref[0] + ahead) % 4
        out_ref[...] = sum(in_ref[y, at].astype(f32) for y in range(4)).astype(bf16)


def line_terms(gathered, place):
    return call(line_terms_kernel, [gathered.shape[2:]] * 4, place.astype(jnp.int32)[None], gathered, flops=64 << 30)


def shifted(terms, axis):
    return [terms[0]] + [shift(terms[ahead], axis, ahead, 4) for ahead in (1, 2, 3)]


def sum_kernel(*refs):
    refs[-1][...] = sum(ref[...].astype(f32) for ref in refs[:-1]).astype(bf16)


def shares_kernel(mlp_ref, *refs):
    out_ref = refs[-1]
    total = sum(ref[...].astype(f32) for ref in refs[:-1]).astype(bf16)
    rows = out_ref.shape[1]
    for member in range(MEMBERS):
        out_ref[member, :, :640] = total[rows * member : rows * (member + 1)]
        out_ref[member, :, 640:] = mlp_ref[rows * member : rows * (member + 1), :]


def ring_terms_kernel(place_ref, *refs):
    for ahead, out_ref in enumerate(refs[4:]):
        at = (place_ref[0] + ahead) % 4
        out_ref[...] = sum(ref[at].astype(f32) for ref in refs[:4]).astype(bf16)


def unpack_kernel(part, in_ref, gate_ref, up_ref, down_ref, query_ref, key_ref, value_ref):
    for member in range(MEMBERS):
        for place, out_ref in enumerate((gate_ref, up_ref, down_ref)):
            at = 640 + part * place
            out_ref[:, part * member : part * (member + 1)] = in_ref[member, :, at : at + part].astype(f32)
    for own in range(4):
        total = in_ref[own, :, :640].astype(f32) + in_ref[own + 4, :, :640].astype(f32)
        query_ref[:, 512 * own : 512 * (own + 1)] = total[:, :512]
        key_ref[:, HEAD_DIM * own : HEAD_DIM * (own + 1)] = total[:, 512 : 512 + HEAD_DIM]
        value_ref[:, HEAD_DIM * own : HEAD_DIM * (own + 1)] = total[:, 512 + HEAD_DIM :]


def attn_pack_kernel(query_ref, key_ref, value_ref, gains_ref, out_ref):
    for member in range(MEMBERS):
        own = member % 4
        out_ref[member, :, :512] = query_ref[:, 512 * own : 512 * (own + 1)]
        out_ref[member, :, 512:640] = jnp.concatenate([head(key_ref, own), head(value_ref, own)], axis=1)
        out_ref[member, :, 640:768] = gains_ref[...]


def mlp_pack_kernel(part, gate_ref, up_ref, down_ref, out_ref):
    for member in range(MEMBERS):
        for place, ref in enumerate((gate_ref, up_ref, down_ref)):
            out_ref[member, :, part * place : part * (place + 1)] = ref[:, part * member : part * (member + 1)]


def rotary_tables():
    half = HEAD_DIM // 2
    frequency = 10000.0 ** (-2.0 * np.arange(half) / HEAD_DIM)
    places = np.arange(LENGTH + HALF) % LENGTH
    angles = np.tile(places[:, None] * frequency[None, :], (1, 4))
    return np.cos(angles).astype(np.float32), np.sin(angles).astype(np.float32)


def on_device(
    tokens, gain_attn, w_query, w_key, w_value, w_out, gain_mlp, w_gate, w_up, w_down, cotangent
):
    own_rows = w_query.shape[0]
    part = w_gate.shape[1] // MEMBERS

    gains = jnp.pad(jnp.concatenate([gain_attn, gain_mlp])[None, :], ((0, own_rows - 1), (0, 128 - 2 * own_rows)))
    block = call(attn_pack_kernel, [(MEMBERS, own_rows, 768)], w_query, w_key, w_value, gains)[0]
    out_block = regroup(w_out)
    block, here, there = together(
        lax.all_to_all(block, GROUP, 0, 0, tiled=True),
        lax.ppermute(out_block, FSDP, head_rows(0)),
        lax.ppermute(out_block, FSDP, head_rows(1)),
    )
    left = lax.axis_index("xl") == 0
    out_block = jnp.concatenate([jnp.where(left, here, there), jnp.where(left, there, here)], axis=0)
    gains = block[:, 0, 640 : 640 + 2 * own_rows].reshape(MEMBERS, 2, own_rows).swapaxes(0, 1).reshape(1, 256)
    gains = jnp.pad(gains, ((0, 2 * own_rows - 1), (0, 256)))
    attn_block = jnp.concatenate(
        [block[:, :, :640].reshape(MEMBERS * own_rows, 640)]
        + [out_block[:, 640 * j : 640 * (j + 1)] for j in range(3)]
        + [jnp.concatenate([out_block[:, 1920:], gains], axis=1)],
        axis=0,
    )
    mlp_block = call(functools.partial(mlp_pack_kernel, part), [(MEMBERS, own_rows, 3 * part)], w_gate, w_up, w_down)[0]
    mlp_block, attn_block = together(mlp_block, attn_block)
    attn_full = lax.all_gather(attn_block, PLANE, axis=0)
    own_tokens, own_cotangent = regroup(tokens[0]), regroup(cotangent[0])
    mlp_block, there_tokens, own_cotangent = together(
        lax.all_to_all(mlp_block, GROUP, 0, 0, tiled=True), shift(own_tokens, "xh", 1, 2), own_cotangent
    )
    mlp_block = mlp_block.reshape(MEMBERS * own_rows, 3 * part)
    mlp_w = lax.all_gather(mlp_block, PLANE, axis=0, tiled=True)

    pair_tokens = (own_tokens, there_tokens), (to_other_core(own_tokens), to_other_core(there_tokens))
    attn_full, pair_tokens, group_cotangent = together(attn_full, pair_tokens, group_gather(own_cotangent))
    gain_one, gain_two = call(gains_kernel, [((1, 2048), f32)] * 2, attn_full, held=(0,))

    first = (HALF * lax.axis_index("xh")).astype(jnp.int32)[None]
    cosine, sine = rotary_tables()

    def attend(chunks):
        shapes = [(LENGTH, 2048), (LENGTH, 640), (LENGTH, 512), (LENGTH, 2048)]
        return call(attend_kernel, shapes, first, *chunks, attn_full, cosine, sine, held=(3,))

    xn_other, qkv_other, mixed_other, out_other = attend(pair_tokens[1])
    xn_own, qkv_own, mixed_own, out_own = attend(pair_tokens[0])
    kept, sent = split_sum(out_own, to_other_core(out_other))
    resid, xn_rows = call(
        resid_kernel, [((HALF, 2048), f32), (HALF, 2048)], own_tokens, kept, shift(sent, "xh", 1, 2), gain_two
    )

    def feed_forward(chip):
        shapes = [(LENGTH, part), (LENGTH, 2 * part), (HALF, 2048), (HALF, 2048)]
        return call(functools.partial(mlp_kernel, part), shapes, *xn_two[chip], *group_cotangent[chip], mlp_w, held=(4,), flops=M_FLOPS)

    arrived = together(*(shift(xn_rows, CHIP_X, -ahead, 4) for ahead in (1, 2, 3)))
    xn_two = [(rows, to_other_core(rows)) for rows in (xn_rows, *arrived)]
    results, got = [None] * 4, [None] * 4

    def core_total(ahead):
        return (results[ahead][2].astype(f32) + to_other_core(results[ahead][3]).astype(f32)).astype(bf16)

    results[2] = feed_forward(2)
    results[3] = feed_forward(3)
    far, xn_one_ahead = together(core_total(2), xn_two[1][0])
    xn_two[1] = xn_one_ahead, xn_two[1][1]
    results[1] = feed_forward(1)
    near, xn_own_rows = together(core_total(3), xn_rows)
    xn_two[0] = xn_own_rows, xn_two[0][1]
    got[3] = shift(near, CHIP_X, 3, 4)
    results[0], got[2] = together(feed_forward(0), shift(far, CHIP_X, 2, 4))
    got[1] = shift(core_total(1), CHIP_X, 1, 4)
    hidden, grad_wide, backs, back_others = (list(kind) for kind in zip(*results))
    flat = [[block for pair in pairs for block in pair] for pairs in (xn_two, group_cotangent)]
    own_other, got[1], got[3], mlp_term = together(
        to_other_core(back_others[0]), got[1], got[3], mlp_terms(part, *flat, grad_wide, hidden)
    )
    shares = lax.psum_scatter(mlp_term, PLANE, scatter_dimension=0, tiled=True)
    grad_resid, grad_rows = call(
        grad_resid_kernel,
        [((HALF, 2048), f32), (HALF, 2048)],
        *(resid, gain_two, own_cotangent, backs[0], own_other, *got[1:]),
    )
    grad_rows, hidden[0] = together(grad_rows, hidden[0])
    out_own, out_other = call(functools.partial(mlp_out_kernel, part), [(4 * HALF, 2048)] * 2, *hidden, mlp_w)
    grad_there, grad_rows_other, out_own, out_other = together(
        shift(grad_rows, "xh", 1, 2), to_other_core(grad_rows), out_own, out_other
    )
    grad_attn = (grad_rows, grad_there), (grad_rows_other, to_other_core(grad_there))

    def attend_back(chunks, qkv):
        shapes = [(LENGTH, 640), (LENGTH, 2048)]
        return call(attend_back_kernel, shapes, first, *chunks, attn_full, cosine, sine, qkv, held=(3,))

    (grad_own, back_own), other_chunks, (out_kept, *out_sent) = together(
        attend_back(grad_attn[0], qkv_own), grad_attn[1], split_sum(out_own, to_other_core(out_other))
    )
    grad_other, back_other = attend_back(other_chunks, qkv_other)
    attn_term = qkv_terms((xn_own, xn_other), (grad_own, grad_other)).reshape(4, 4, 8 * own_rows, 640)
    attn_term, back_own, grad_attn = together(attn_term, back_own, grad_attn)
    kept, sent = split_sum(back_own, to_other_core(back_other))
    out_term = out_terms(lax.axis_index("z"), (mixed_own, mixed_other), grad_attn)
    out_got = [shift(rows, CHIP_X, ahead, 4) for ahead, rows in zip((1, 2, 3), out_sent)]
    grad_got = shift(sent, "xh", 1, 2)
    place_y = lax.axis_index("y").astype(jnp.int32)[None]
    attn_terms, out_term, out_got = together(
        line_terms(lax.all_to_all(attn_term, "y", 0, 0, tiled=True), lax.axis_index("z")),
        shifted(out_term, "z"),
        out_got,
    )
    shares = call(
        shares_kernel, [(MEMBERS, own_rows, 640 + 3 * part)], shares, *shifted(attn_terms, "z")
    )[0]
    block_output = call(block_output_kernel, [(HALF, 2048)], resid, out_kept, *out_got)[0]
    shares, out_term, grad_got, block_output = together(shares, out_term, grad_got, block_output)
    out_term = call(ring_terms_kernel, [(2 * own_rows, 2048)] * 4, place_y, *out_term)
    out_share = call(sum_kernel, [(2 * own_rows, 2048)], *shifted(out_term, "y"))[0]
    input_grad = call(input_grad_kernel, [((HALF, 2048), f32)], own_tokens, gain_one, grad_resid, kept, grad_got)[0]
    taken = jnp.where(left, out_share[:own_rows], out_share[own_rows:])
    given = jnp.where(left, out_share[own_rows:], out_share[:own_rows])
    taken = lax.ppermute(taken, FSDP, back_rows(0))
    given = lax.ppermute(given, FSDP, back_rows(1))
    shares, block_output, input_grad = together(
        call(
            functools.partial(unpack_kernel, part),
            [((own_rows, MEMBERS * part), f32)] * 3
            + [((own_rows, 2048), f32), ((own_rows, 256), f32), ((own_rows, 256), f32)],
            lax.all_to_all(shares, GROUP, 0, 0, tiled=True),
            flops=64 << 30,
        ),
        block_output,
        input_grad,
    )
    gate_grad, up_grad, down_grad, query_grad, key_grad, value_grad = shares
    def gain_grad(gain, *pairs):
        total = sum(jnp.sum(w.astype(f32) * grad, axis=1) for w, grad in pairs)
        return total / gain.astype(f32)

    gain_attn_grad = gain_grad(gain_attn, (w_query, query_grad), (w_key, key_grad), (w_value, value_grad))
    gain_mlp_grad = gain_grad(gain_mlp, (w_gate, gate_grad), (w_up, up_grad))
    gain_attn_grad, gain_mlp_grad, taken, given = together(gain_attn_grad, gain_mlp_grad, taken, given)
    out_grad = call(out_grad_kernel, [((own_rows, 2048), f32)], taken, given)[0]
    return (
        block_output[None],
        input_grad[None],
        gain_attn_grad,
        query_grad,
        key_grad,
        value_grad,
        out_grad,
        gain_mlp_grad,
        gate_grad,
        up_grad,
        down_grad,
    )


def solution(mesh):
    view = Mesh(mesh.devices.reshape(SIZES), AXES)
    split = P(("xh",) + FSDP)
    rows = P(("xh",) + FSDP, None)
    data = P(FSDP, "xh", None)
    return jax.shard_map(
        on_device,
        mesh=view,
        in_specs=(data, split, rows, rows, rows, rows, split, rows, rows, rows, data),
        out_specs=(data, data, split, rows, rows, rows, rows, split, rows, rows, rows),
        check_vma=False,
    )
```

```python
import functools

import jax
import jax.numpy as jnp
import numpy as np
from jax import lax
from jax.experimental import pallas as pl
from jax.experimental.pallas import tpu as pltpu
from jax.sharding import Mesh, PartitionSpec as P

HEADS = 32
KV_HEADS = 4
HEAD_DIM = 64
EPS = 1e-05
NEG = -1e30
LENGTH = 256
HALF = 128
MIB = 1024 * 1024
M_FLOPS = 1 << 20

AXES = ("xh", "y", "z", "xl", "c")
SIZES = (2, 4, 4, 2, 2)
CHIP_X = ("xh", "xl")
GROUP = ("xl", "xh", "c")
MEMBERS = 8
PAIRED = ("xh", "c")
PLANE = ("y", "z")

bf16 = jnp.bfloat16
f32 = jnp.float32


def contract(a, b, dim_a, dim_b):
    return lax.dot_general(a, b, (((dim_a,), (dim_b,)), ((), ())), preferred_element_type=f32)


def shift(values, axis, by, size):
    return lax.ppermute(values, axis, [(i, (i + by) % size) for i in range(size)])


def together(*values):
    return lax.optimization_barrier(values)


def regroup_to(out_ref, values):
    for k in range(16):
        low = values[:, 64 * k : 64 * k + 64]
        high = values[:, 1024 + 64 * k : 1088 + 64 * k]
        out_ref[:, 128 * k : 128 * (k + 1)] = jnp.concatenate(
            [low[:, :32], high[:, :32], low[:, 32:], high[:, 32:]], axis=1
        )


def regroup_back_to(out_ref, values):
    for k in range(16):
        tile = values[:, 128 * k : 128 * (k + 1)]
        out_ref[:, 64 * k : 64 * k + 64] = jnp.concatenate([tile[:, :32], tile[:, 64:96]], axis=1)
        out_ref[:, 1024 + 64 * k : 1088 + 64 * k] = jnp.concatenate([tile[:, 32:64], tile[:, 96:]], axis=1)


def regroup_kernel(in_ref, out_ref):
    regroup_to(out_ref, in_ref[...])


def regroup(values):
    return call(regroup_kernel, [values.shape], values)[0]


def to_other_core(rows):
    return shift(rows, "c", 1, 2)


def split_sum_kernel(own_ref, got_ref, kept_ref, *sent_refs):
    total = own_ref[...].astype(f32) + got_ref[...].astype(f32)
    rows = kept_ref.shape[0]
    kept_ref[...] = total[:rows]
    for at, sent_ref in enumerate(sent_refs):
        sent_ref[...] = total[rows * (at + 1) : rows * (at + 2)].astype(bf16)


def split_sum(own, got):
    rows, width = HALF, own.shape[1]
    return call(split_sum_kernel, [((rows, width), f32)] + [(rows, width)] * (own.shape[0] // rows - 1), own, got)


def group_gather(rows):
    own = (rows, *together(*(shift(rows, CHIP_X, -ahead, 4) for ahead in (1, 2, 3))))
    return [(block, to_other_core(block)) for block in own]


def line_sum(terms, axis):
    return jnp.sum(lax.all_to_all(terms, axis, 0, 0, tiled=True).astype(f32), axis=0)


def head_rows(flip):
    pairs = []
    for a in range(2):
        for b in range(2):
            for z in range(4):
                for xl in range(2):
                    for c in range(2):
                        source = (((2 * a + b) * 4 + z) * 2 + xl) * 2 + c
                        to_y, to_z = 2 * b + z // 2, 2 * (z % 2) + xl
                        pairs.append((source, ((to_y * 4 + to_z) * 2 + (c ^ flip)) * 2 + a))
    return pairs


def back_rows(flip):
    return [(there, here) for here, there in head_rows(flip)]


FSDP = ("y", "z", "xl", "c")


def rms_scale(values):
    return lax.rsqrt(jnp.mean(values * values, axis=1, keepdims=True) + EPS)


def norm_back(grad_normed, normed, scale_rows, gain):
    scaled = grad_normed * gain
    return scale_rows * (scaled - normed * jnp.mean(scaled * normed, axis=1, keepdims=True))


def resid_kernel(tokens_ref, kept_ref, got_ref, gain_ref, resid_ref, xn_ref):
    resid = tokens_ref[...].astype(f32) + kept_ref[...] + got_ref[...].astype(f32)
    resid_ref[...] = resid
    xn_ref[...] = (resid * rms_scale(resid) * gain_ref[...]).astype(bf16)


def grad_resid_kernel(resid_ref, gain_ref, cot_ref, own_ref, other_ref, *refs):
    grad = own_ref[...].astype(f32) + other_ref[...].astype(f32) + sum(ref[...].astype(f32) for ref in refs[:3])
    resid = resid_ref[...]
    scale = rms_scale(resid)
    grad = cot_ref[...].astype(f32) + norm_back(grad, resid * scale, scale, gain_ref[...])
    refs[3][...] = grad
    refs[4][...] = grad.astype(bf16)


def input_grad_kernel(tokens_ref, gain_ref, grad_resid_ref, kept_ref, got_ref, out_ref):
    inputs = tokens_ref[...].astype(f32)
    scale = rms_scale(inputs)
    grad = kept_ref[...] + got_ref[...].astype(f32)
    regroup_back_to(out_ref, grad_resid_ref[...] + norm_back(grad, inputs * scale, scale, gain_ref[...]))


def block_output_kernel(resid_ref, kept_ref, *refs):
    out = resid_ref[...] + kept_ref[...] + sum(ref[...].astype(f32) for ref in refs[:3])
    regroup_back_to(refs[3], out.astype(bf16))


def out_grad_kernel(kept_ref, given_ref, out_ref):
    regroup_back_to(out_ref, kept_ref[...].astype(f32) + given_ref[...].astype(f32))


def rotate_half(values):
    width = values.shape[1]
    lane = lax.broadcasted_iota(jnp.int32, values.shape, 1) % HEAD_DIM
    later = pltpu.roll(values, width - HEAD_DIM // 2, 1)
    earlier = pltpu.roll(values, HEAD_DIM // 2, 1)
    return jnp.where(lane < HEAD_DIM // 2, -later, earlier)


def head(values, h):
    return values[:, HEAD_DIM * h : HEAD_DIM * (h + 1)]


def allowed_places(first):
    shape = (LENGTH, LENGTH)
    rows = (lax.broadcasted_iota(jnp.int32, shape, 0) + first) & (LENGTH - 1)
    return ((lax.broadcasted_iota(jnp.int32, shape, 1) + first) & (LENGTH - 1)) <= rows


def probabilities(query, key, allowed):
    scores = jnp.where(allowed, contract(query, key, 1, 1) * HEAD_DIM**-0.5, NEG)
    exp_scores = jnp.exp(scores - jnp.max(scores, axis=1, keepdims=True))
    return exp_scores / jnp.sum(exp_scores, axis=1, keepdims=True)


def wide_table(ref, first, width):
    rows = ref[pl.ds(pl.multiple_of(first, HALF), LENGTH), :]
    return jnp.concatenate([rows] * (width // 128), axis=1)


def out_weights(full_ref):
    for j in range(4):
        width = min(640, 2048 - 640 * j)
        yield full_ref[:, 128 + 32 * j : 160 + 32 * j, :width].reshape(512, width), 640 * j, width


def gain_row(full_ref, which):
    at = 128 * (which + 1)
    return jnp.concatenate([full_ref[y, 224:240, at : at + 128].astype(f32)[:1] for y in range(16)], axis=1)


def gains_kernel(full_ref, *out_refs):
    for which, out_ref in enumerate(out_refs):
        out_ref[...] = gain_row(full_ref, which)


def attend_kernel(first_ref, own_ref, there_ref, full_ref, cos_ref, sin_ref, xn_ref, qkv_ref, mixed_ref, out_ref):
    first = first_ref[0]
    cosine, sine = wide_table(cos_ref, first, 512), wide_table(sin_ref, first, 512)
    inputs = jnp.concatenate([own_ref[...], there_ref[...]], axis=0).astype(f32)
    xn_ref[...] = (inputs * rms_scale(inputs) * gain_row(full_ref, 0)).astype(bf16)
    proj = contract(xn_ref[...], full_ref[:, :128, :].reshape(2048, 640), 1, 0).astype(bf16)
    query = proj[:, :512].astype(f32)
    query = (query * cosine + rotate_half(query) * sine).astype(bf16)
    qkv_ref[:, :512] = query
    wide = proj[:, 512:].astype(f32)
    turned = wide * cosine[:, :128] + rotate_half(wide) * sine[:, :128]
    lane = lax.broadcasted_iota(jnp.int32, wide.shape, 1)
    key_value = jnp.where(lane < HEAD_DIM, turned, wide).astype(bf16)
    qkv_ref[:, 512:] = key_value
    key, value = key_value[:, :HEAD_DIM], key_value[:, HEAD_DIM:]
    allowed = allowed_places(first)
    mixed = [
        contract(probabilities(head(query, h), key, allowed).astype(bf16), value, 1, 0) for h in range(8)
    ]
    mixed_ref[...] = jnp.concatenate(mixed, axis=1).astype(bf16)
    for weights, at, width in out_weights(full_ref):
        out_ref[:, at : at + width] = contract(mixed_ref[...], weights, 1, 0).astype(bf16)


def attend_back_kernel(first_ref, own_ref, there_ref, full_ref, cos_ref, sin_ref, qkv_ref, out_ref, back_ref):
    first = first_ref[0]
    cosine, sine = wide_table(cos_ref, first, 512), wide_table(sin_ref, first, 512)
    grad = jnp.concatenate([own_ref[...], there_ref[...]], axis=0)
    grad = sum(contract(grad[:, at : at + width], weights, 1, 1) for weights, at, width in out_weights(full_ref))
    grad = grad.astype(bf16)
    query = qkv_ref[:, :512]
    key_value = qkv_ref[:, 512:]
    key, value = key_value[:, :HEAD_DIM], key_value[:, HEAD_DIM:]
    allowed = allowed_places(first)
    grad_key = jnp.zeros((LENGTH, HEAD_DIM), f32)
    grad_value = jnp.zeros((LENGTH, HEAD_DIM), f32)
    grad_query = []
    for h in range(8):
        probs = probabilities(head(query, h), key, allowed)
        grad_probs = contract(head(grad, h), value, 1, 1)
        delta = jnp.sum(probs * grad_probs, axis=1, keepdims=True)
        grad_scores = (probs * (grad_probs - delta)).astype(bf16)
        grad_query.append(contract(grad_scores, key, 1, 0))
        grad_key = grad_key + contract(grad_scores, head(query, h), 0, 0)
        grad_value = grad_value + contract(probs.astype(bf16), head(grad, h), 0, 0)
    grad_query = jnp.concatenate(grad_query, axis=1) * HEAD_DIM**-0.5
    out_ref[:, :512] = (grad_query * cosine - rotate_half(grad_query * sine)).astype(bf16)
    wide = jnp.concatenate([grad_key * HEAD_DIM**-0.5, grad_value], axis=1)
    turned = wide * cosine[:, :128] - rotate_half(wide * sine[:, :128])
    lane = lax.broadcasted_iota(jnp.int32, wide.shape, 1)
    out_ref[:, 512:] = jnp.where(lane < HEAD_DIM, turned, wide).astype(bf16)
    back_ref[...] = contract(out_ref[...], full_ref[:, :128, :].reshape(2048, 640), 1, 1).astype(bf16)


def call(kernel, outs, *arrays, grid=(), in_specs=None, out_specs=None, hbm=False, held=(), flops=1 << 20, scratch=(), vmem_mib=12):
    kind = pltpu.HBM if hbm else jax.ShapeDtypeStruct
    outs = [out if isinstance(out[1], type) or hasattr(out[1], "dtype") else (out, bf16) for out in outs]
    vmem, smem, block = pl.BlockSpec(memory_space=pltpu.VMEM), pl.BlockSpec(memory_space=pltpu.SMEM), pl.BlockSpec()
    if in_specs is None:
        in_specs = [smem if a.dtype == jnp.int32 else vmem if at in held else block for at, a in enumerate(arrays)]
    return pl.pallas_call(
        kernel,
        out_shape=[kind(shape, dtype) for shape, dtype in outs],
        grid=grid,
        in_specs=in_specs,
        out_specs=out_specs or [block] * len(outs),
        scratch_shapes=scratch,
        compiler_params=pltpu.CompilerParams(vmem_limit_bytes=vmem_mib * MIB),
        cost_estimate=pl.CostEstimate(flops=flops, bytes_accessed=1024, transcendentals=0),
    )(*arrays)


def mlp_kernel(part, own_ref, other_ref, own_cot_ref, other_cot_ref, w_ref, hidden_ref, grad_ref, back_ref, back_other_ref):
    xn = jnp.concatenate([own_ref[...], other_ref[...]], axis=0)
    cot = jnp.concatenate([own_cot_ref[...], other_cot_ref[...]], axis=0)
    wide = contract(xn, w_ref[:, : 2 * part], 1, 0)
    grad_hidden = contract(cot, w_ref[:, 2 * part :], 1, 0)
    gate, up = wide[:, :part], wide[:, part:]
    sigmoid_gate = jax.nn.sigmoid(gate)
    silu_gate = gate * sigmoid_gate
    hidden_ref[...] = (silu_gate * up).astype(bf16)
    grad_ref[:, :part] = (
        grad_hidden * up * (sigmoid_gate * (1.0 + gate * (1.0 - sigmoid_gate)))
    ).astype(bf16)
    grad_ref[:, part:] = (grad_hidden * silu_gate).astype(bf16)
    back = contract(grad_ref[...], w_ref[:, : 2 * part], 1, 1).astype(bf16)
    rows = own_ref.shape[0]
    back_ref[...] = back[:rows]
    back_other_ref[...] = back[rows:]


def mlp_out_kernel(part, *refs):
    hidden_refs, w_ref, out_refs = refs[:4], refs[4], refs[5:]
    for chip in range(4):
        out = contract(hidden_refs[chip][...], w_ref[:, 2 * part :], 1, 1).astype(bf16)
        rows = out.shape[0] // 2
        for core in range(2):
            out_refs[core][rows * chip : rows * (chip + 1), :] = out[rows * core : rows * (core + 1)]


def mlp_terms_kernel(part, *refs):
    xn, cot, grad, hidden = [
        jnp.concatenate([ref[...] for ref in group], axis=0) for group in (refs[:8], refs[8:16], refs[16:20], refs[20:24])
    ]
    out_ref = refs[24]
    out_ref[:, : 2 * part] = contract(xn, grad, 0, 0).astype(bf16)
    out_ref[:, 2 * part :] = contract(cot, hidden, 0, 0).astype(bf16)


def columns_spec(rows, block):
    return pl.BlockSpec((rows, block), lambda i: (0, i))


def whole_spec(array):
    return pl.BlockSpec(array.shape, lambda i: (0, 0), pipeline_mode=pl.Buffered(1))


def mlp_terms(part, xn, cot, grad, hidden):
    rows, width = xn[0].shape
    block = 512
    return call(
        functools.partial(mlp_terms_kernel, part),
        [(width, 3 * part)],
        *xn,
        *cot,
        *grad,
        *hidden,
        grid=(width // block,),
        in_specs=[columns_spec(rows, block)] * 16 + [whole_spec(a) for a in grad + hidden],
        out_specs=[pl.BlockSpec((block, 3 * part), lambda i: (i, 0))],
        hbm=True,
        vmem_mib=24,
    )[0]


def out_terms_kernel(place_ref, mixed_ref, mixed_other_ref, *refs):
    own, other = [jnp.concatenate([ref[...] for ref in pair], axis=0) for pair in (refs[:2], refs[2:4])]
    terms_ref, out_refs = refs[8], refs[4:8]
    terms_ref[...] = (contract(mixed_ref[...], own, 0, 0) + contract(mixed_other_ref[...], other, 0, 0)).astype(bf16)
    for ahead, out_ref in enumerate(out_refs):
        at = (place_ref[0] + ahead) % 4
        for y in range(4):
            out_ref[y] = terms_ref[pl.ds(pl.multiple_of((4 * y + at) * 32, 32), 32), :]


def out_terms(place, mixed, grad):
    rows, width = grad[0][0].shape
    block = 512
    blocks = [columns_spec(rows, block)] * 4
    return call(
        out_terms_kernel,
        [(4, 32, width)] * 4,
        place.astype(jnp.int32)[None],
        *mixed,
        *grad[0],
        *grad[1],
        grid=(width // block,),
        in_specs=[pl.BlockSpec(memory_space=pltpu.SMEM)] + [whole_spec(a) for a in mixed] + blocks,
        out_specs=[pl.BlockSpec((4, 32, block), lambda i: (0, 0, i))] * 4,
        scratch=[pltpu.VMEM((512, block), bf16)],
    )


def qkv_terms_kernel(xn_ref, xn_other_ref, grad_ref, grad_other_ref, out_ref):
    out_ref[...] = (
        contract(xn_ref[...], grad_ref[...], 0, 0) + contract(xn_other_ref[...], grad_other_ref[...], 0, 0)
    ).astype(bf16)


def qkv_terms(xn, grad):
    rows, width = xn[0].shape
    block = 1024
    return call(
        qkv_terms_kernel,
        [(width, 640)],
        *xn,
        *grad,
        grid=(width // block,),
        in_specs=[columns_spec(rows, block)] * 2 + [whole_spec(a) for a in grad],
        out_specs=[pl.BlockSpec((block, 640), lambda i: (i, 0))],
        hbm=True,
    )[0]


def line_terms_kernel(place_ref, in_ref, *out_refs):
    for ahead, out_ref in enumerate(out_refs):
        at = (place_ref[0] + ahead) % 4
        out_ref[...] = sum(in_ref[y, at].astype(f32) for y in range(4)).astype(bf16)


def line_terms(gathered, place):
    return call(line_terms_kernel, [gathered.shape[2:]] * 4, place.astype(jnp.int32)[None], gathered, flops=64 << 30)


def shifted(terms, axis):
    return [terms[0]] + [shift(terms[ahead], axis, ahead, 4) for ahead in (1, 2, 3)]


def sum_kernel(*refs):
    refs[-1][...] = sum(ref[...].astype(f32) for ref in refs[:-1]).astype(bf16)


def shares_kernel(mlp_ref, *refs):
    out_ref = refs[-1]
    total = sum(ref[...].astype(f32) for ref in refs[:-1]).astype(bf16)
    rows = out_ref.shape[1]
    for member in range(MEMBERS):
        out_ref[member, :, :640] = total[rows * member : rows * (member + 1)]
        out_ref[member, :, 640:] = mlp_ref[rows * member : rows * (member + 1), :]


def ring_terms_kernel(place_ref, *refs):
    for ahead, out_ref in enumerate(refs[4:]):
        at = (place_ref[0] + ahead) % 4
        out_ref[...] = sum(ref[at].astype(f32) for ref in refs[:4]).astype(bf16)


def unpack_kernel(part, in_ref, gate_ref, up_ref, down_ref, query_ref, key_ref, value_ref):
    for member in range(MEMBERS):
        for place, out_ref in enumerate((gate_ref, up_ref, down_ref)):
            at = 640 + part * place
            out_ref[:, part * member : part * (member + 1)] = in_ref[member, :, at : at + part].astype(f32)
    for own in range(4):
        total = in_ref[own, :, :640].astype(f32) + in_ref[own + 4, :, :640].astype(f32)
        query_ref[:, 512 * own : 512 * (own + 1)] = total[:, :512]
        key_ref[:, HEAD_DIM * own : HEAD_DIM * (own + 1)] = total[:, 512 : 512 + HEAD_DIM]
        value_ref[:, HEAD_DIM * own : HEAD_DIM * (own + 1)] = total[:, 512 + HEAD_DIM :]


def attn_pack_kernel(query_ref, key_ref, value_ref, gains_ref, out_ref):
    for member in range(MEMBERS):
        own = member % 4
        out_ref[member, :, :512] = query_ref[:, 512 * own : 512 * (own + 1)]
        out_ref[member, :, 512:640] = jnp.concatenate([head(key_ref, own), head(value_ref, own)], axis=1)
        out_ref[member, :, 640:768] = gains_ref[...]


def mlp_pack_kernel(part, gate_ref, up_ref, down_ref, out_ref):
    for member in range(MEMBERS):
        for place, ref in enumerate((gate_ref, up_ref, down_ref)):
            out_ref[member, :, part * place : part * (place + 1)] = ref[:, part * member : part * (member + 1)]


def rotary_tables():
    half = HEAD_DIM // 2
    frequency = 10000.0 ** (-2.0 * np.arange(half) / HEAD_DIM)
    places = np.arange(LENGTH + HALF) % LENGTH
    angles = np.tile(places[:, None] * frequency[None, :], (1, 4))
    return np.cos(angles).astype(np.float32), np.sin(angles).astype(np.float32)


def on_device(
    tokens, gain_attn, w_query, w_key, w_value, w_out, gain_mlp, w_gate, w_up, w_down, cotangent
):
    own_rows = w_query.shape[0]
    part = w_gate.shape[1] // MEMBERS

    gains = jnp.pad(jnp.concatenate([gain_attn, gain_mlp])[None, :], ((0, own_rows - 1), (0, 128 - 2 * own_rows)))
    block = call(attn_pack_kernel, [(MEMBERS, own_rows, 768)], w_query, w_key, w_value, gains)[0]
    out_block = regroup(w_out)
    block, here, there = together(
        lax.all_to_all(block, GROUP, 0, 0, tiled=True),
        lax.ppermute(out_block, FSDP, head_rows(0)),
        lax.ppermute(out_block, FSDP, head_rows(1)),
    )
    left = lax.axis_index("xl") == 0
    out_block = jnp.concatenate([jnp.where(left, here, there), jnp.where(left, there, here)], axis=0)
    gains = block[:, 0, 640 : 640 + 2 * own_rows].reshape(MEMBERS, 2, own_rows).swapaxes(0, 1).reshape(1, 256)
    gains = jnp.pad(gains, ((0, 2 * own_rows - 1), (0, 256)))
    attn_block = jnp.concatenate(
        [block[:, :, :640].reshape(MEMBERS * own_rows, 640)]
        + [out_block[:, 640 * j : 640 * (j + 1)] for j in range(3)]
        + [jnp.concatenate([out_block[:, 1920:], gains], axis=1)],
        axis=0,
    )
    mlp_block = call(functools.partial(mlp_pack_kernel, part), [(MEMBERS, own_rows, 3 * part)], w_gate, w_up, w_down)[0]
    mlp_block, attn_block = together(mlp_block, attn_block)
    attn_full = lax.all_gather(attn_block, PLANE, axis=0)
    own_tokens, own_cotangent = regroup(tokens[0]), regroup(cotangent[0])
    mlp_block, there_tokens, own_cotangent = together(
        lax.all_to_all(mlp_block, GROUP, 0, 0, tiled=True), shift(own_tokens, "xh", 1, 2), own_cotangent
    )
    mlp_block = mlp_block.reshape(MEMBERS * own_rows, 3 * part)
    mlp_w = lax.all_gather(mlp_block, PLANE, axis=0, tiled=True)

    pair_tokens = (own_tokens, there_tokens), (to_other_core(own_tokens), to_other_core(there_tokens))
    attn_full, pair_tokens, group_cotangent = together(attn_full, pair_tokens, group_gather(own_cotangent))
    gain_one, gain_two = call(gains_kernel, [((1, 2048), f32)] * 2, attn_full, held=(0,))

    first = (HALF * lax.axis_index("xh")).astype(jnp.int32)[None]
    cosine, sine = rotary_tables()

    def attend(chunks):
        shapes = [(LENGTH, 2048), (LENGTH, 640), (LENGTH, 512), (LENGTH, 2048)]
        return call(attend_kernel, shapes, first, *chunks, attn_full, cosine, sine, held=(3,))

    xn_other, qkv_other, mixed_other, out_other = attend(pair_tokens[1])
    xn_own, qkv_own, mixed_own, out_own = attend(pair_tokens[0])
    kept, sent = split_sum(out_own, to_other_core(out_other))
    resid, xn_rows = call(
        resid_kernel, [((HALF, 2048), f32), (HALF, 2048)], own_tokens, kept, shift(sent, "xh", 1, 2), gain_two
    )

    def feed_forward(chip):
        shapes = [(LENGTH, part), (LENGTH, 2 * part), (HALF, 2048), (HALF, 2048)]
        return call(functools.partial(mlp_kernel, part), shapes, *xn_two[chip], *group_cotangent[chip], mlp_w, held=(4,), flops=M_FLOPS)

    arrived = together(*(shift(xn_rows, CHIP_X, -ahead, 4) for ahead in (1, 2, 3)))
    xn_two = [(rows, to_other_core(rows)) for rows in (xn_rows, *arrived)]
    results, got = [None] * 4, [None] * 4

    def core_total(ahead):
        return (results[ahead][2].astype(f32) + to_other_core(results[ahead][3]).astype(f32)).astype(bf16)

    results[2] = feed_forward(2)
    results[3] = feed_forward(3)
    far, xn_one_ahead = together(core_total(2), xn_two[1][0])
    xn_two[1] = xn_one_ahead, xn_two[1][1]
    results[1] = feed_forward(1)
    near, xn_own_rows = together(core_total(3), xn_rows)
    xn_two[0] = xn_own_rows, xn_two[0][1]
    got[3] = shift(near, CHIP_X, 3, 4)
    results[0], got[2] = together(feed_forward(0), shift(far, CHIP_X, 2, 4))
    got[1] = shift(core_total(1), CHIP_X, 1, 4)
    hidden, grad_wide, backs, back_others = (list(kind) for kind in zip(*results))
    flat = [[block for pair in pairs for block in pair] for pairs in (xn_two, group_cotangent)]
    own_other, got[1], got[3], mlp_term = together(
        to_other_core(back_others[0]), got[1], got[3], mlp_terms(part, *flat, grad_wide, hidden)
    )
    shares = lax.psum_scatter(mlp_term, PLANE, scatter_dimension=0, tiled=True)
    grad_resid, grad_rows = call(
        grad_resid_kernel,
        [((HALF, 2048), f32), (HALF, 2048)],
        *(resid, gain_two, own_cotangent, backs[0], own_other, *got[1:]),
    )
    grad_rows, hidden[0] = together(grad_rows, hidden[0])
    out_own, out_other = call(functools.partial(mlp_out_kernel, part), [(4 * HALF, 2048)] * 2, *hidden, mlp_w, vmem_mib=20)
    grad_there, grad_rows_other, out_own, out_other = together(
        shift(grad_rows, "xh", 1, 2), to_other_core(grad_rows), out_own, out_other
    )
    grad_attn = (grad_rows, grad_there), (grad_rows_other, to_other_core(grad_there))

    def attend_back(chunks, qkv):
        shapes = [(LENGTH, 640), (LENGTH, 2048)]
        return call(attend_back_kernel, shapes, first, *chunks, attn_full, cosine, sine, qkv, held=(3,))

    (grad_own, back_own), other_chunks, (out_kept, *out_sent) = together(
        attend_back(grad_attn[0], qkv_own), grad_attn[1], split_sum(out_own, to_other_core(out_other))
    )
    grad_other, back_other = attend_back(other_chunks, qkv_other)
    attn_term = qkv_terms((xn_own, xn_other), (grad_own, grad_other)).reshape(4, 4, 8 * own_rows, 640)
    attn_term, back_own, grad_attn = together(attn_term, back_own, grad_attn)
    kept, sent = split_sum(back_own, to_other_core(back_other))
    out_term = out_terms(lax.axis_index("z"), (mixed_own, mixed_other), grad_attn)
    out_got = [shift(rows, CHIP_X, ahead, 4) for ahead, rows in zip((1, 2, 3), out_sent)]
    grad_got = shift(sent, "xh", 1, 2)
    place_y = lax.axis_index("y").astype(jnp.int32)[None]
    attn_terms, out_term, out_got = together(
        line_terms(lax.all_to_all(attn_term, "y", 0, 0, tiled=True), lax.axis_index("z")),
        shifted(out_term, "z"),
        out_got,
    )
    shares = call(
        shares_kernel, [(MEMBERS, own_rows, 640 + 3 * part)], shares, *shifted(attn_terms, "z")
    )[0]
    block_output = call(block_output_kernel, [(HALF, 2048)], resid, out_kept, *out_got)[0]
    shares, out_term, grad_got, block_output = together(shares, out_term, grad_got, block_output)
    out_term = call(ring_terms_kernel, [(2 * own_rows, 2048)] * 4, place_y, *out_term)
    out_share = call(sum_kernel, [(2 * own_rows, 2048)], *shifted(out_term, "y"))[0]
    input_grad = call(input_grad_kernel, [((HALF, 2048), f32)], own_tokens, gain_one, grad_resid, kept, grad_got)[0]
    taken = jnp.where(left, out_share[:own_rows], out_share[own_rows:])
    given = jnp.where(left, out_share[own_rows:], out_share[:own_rows])
    taken = lax.ppermute(taken, FSDP, back_rows(0))
    given = lax.ppermute(given, FSDP, back_rows(1))
    shares, block_output, input_grad = together(
        call(
            functools.partial(unpack_kernel, part),
            [((own_rows, MEMBERS * part), f32)] * 3
            + [((own_rows, 2048), f32), ((own_rows, 256), f32), ((own_rows, 256), f32)],
            lax.all_to_all(shares, GROUP, 0, 0, tiled=True),
            flops=64 << 30,
        ),
        block_output,
        input_grad,
    )
    gate_grad, up_grad, down_grad, query_grad, key_grad, value_grad = shares
    def gain_grad(gain, *pairs):
        total = sum(jnp.sum(w.astype(f32) * grad, axis=1) for w, grad in pairs)
        return total / gain.astype(f32)

    gain_attn_grad = gain_grad(gain_attn, (w_query, query_grad), (w_key, key_grad), (w_value, value_grad))
    gain_mlp_grad = gain_grad(gain_mlp, (w_gate, gate_grad), (w_up, up_grad))
    gain_attn_grad, gain_mlp_grad, taken, given = together(gain_attn_grad, gain_mlp_grad, taken, given)
    out_grad = call(out_grad_kernel, [((own_rows, 2048), f32)], taken, given)[0]
    return (
        block_output[None],
        input_grad[None],
        gain_attn_grad,
        query_grad,
        key_grad,
        value_grad,
        out_grad,
        gain_mlp_grad,
        gate_grad,
        up_grad,
        down_grad,
    )


def solution(mesh):
    view = Mesh(mesh.devices.reshape(SIZES), AXES)
    split = P(("xh",) + FSDP)
    rows = P(("xh",) + FSDP, None)
    data = P(FSDP, "xh", None)
    return jax.shard_map(
        on_device,
        mesh=view,
        in_specs=(data, split, rows, rows, rows, rows, split, rows, rows, rows, data),
        out_specs=(data, data, split, rows, rows, rows, rows, split, rows, rows, rows),
        check_vma=False,
    )
```
